512 devices in a mesh: sec: 64 (over x, y, core), term: 8 (over z).
Axes of the slice: x: 4, y: 8, z: 8, core: 2. Of those that a mesh axis runs over, the one named last changes fastest.
Arguments:
- wavefunction: bfloat16 [64, 64, 128, 128], P('sec'), may hold values from -6 to 6
- left_env: bfloat16 [8, 5, 64, 128, 128], P('term', None, 'sec'), may hold values from -0.5 to 0.5
- right_env: bfloat16 [8, 64, 128, 128], P('term', 'sec'), may hold values from -0.5 to 0.5
- coupling: float32 [8, 5, 64, 64], P('term'), may hold values from -1 to 1
- left_shift: int32 [8, 5], P('term'), may hold values from -1 to 1
- allowed: int32 [64, 64], replicated, may hold values 0 or 1
Outputs:
- applied: bfloat16 [64, 64, 128, 128], P('term', 'sec')
The draws below stay inside these ranges and needn't reach their ends.
All inputs are finite; a program needn't handle non-finite values.
Results may differ from the reference program's by a relative error of at most 0.0049.
Values may be sent and summed in bfloat16 or wider, within the bound.
No kernel may reach another device: no remote copies, remote signals or barrier semaphores. Data moves between devices by JAX's collectives and lax.ppermute only.
A program may use at most 128 MiB of HBM per device.

```python
import jax
import jax.numpy as jnp
from jax import lax

M = 128
LB = 5
NS = 64
NW = 8


def with_ends(values, rng, low, largest):
    longest = values.shape.index(max(values.shape))
    spots = []
    for shift in (0, 1):
        where = [jax.random.randint(jax.random.fold_in(rng, axis), (), 0, length) for axis, length in enumerate(values.shape)]
        where[longest] = (where[longest] + shift) % values.shape[longest]
        spots.append(tuple(where))
    return values.at[spots[0]].set(low).at[spots[1]].set(largest)


def shard_levels(key, extent, cuts, least, high):
    factor_of, own = 1.0, jax.random.fold_in(key, 6)
    for axis_at, parts in cuts:
        steps = jnp.exp(jax.random.uniform(jax.random.fold_in(own, axis_at), (parts,), jnp.float32, least / len(cuts), high / len(cuts)))
        factor_of = factor_of * jnp.repeat(steps, extent[axis_at] // parts).reshape([-1 if axis == axis_at else 1 for axis in range(len(extent))])
    return factor_of


def noise(stream_key, shape, width, limit, split=(), kind=jnp.bfloat16):
    entries = jax.random.normal(stream_key, shape, jnp.float32) * width
    if len(split) > 0:
        entries = shard_levels(stream_key, shape, split, -0.22, 0.18) * entries
    return jnp.clip(entries, min=-limit, max=limit).astype(kind)


def setup_inputs(seed: int = 0) -> dict:
    key_list = jax.random.split(jax.random.key(seed), 7)
    return {
        "wavefunction": noise(key_list[0], (NS, NS, M, M), 1.0, 6.0, ((0, 64),)),
        "left_env": noise(key_list[1], (NW, LB, NS, M, M), M ** -0.5, 0.5, ((0, 8), (2, 64))),
        "right_env": noise(key_list[2], (NW, NS, M, M), M ** -0.5, 0.5, ((0, 8), (1, 64))),
        "coupling": noise(key_list[3], (NW, LB, NS, NS), (NW * LB) ** -0.5, 1.0, ((0, 8),), jnp.float32),
        "left_shift": with_ends(jax.random.randint(key_list[4], (NW, LB), -1, 2), jax.random.fold_in(key_list[4], 1), -1, 1).astype(jnp.int32),
        "allowed": with_ends((jax.random.randint(key_list[5], (NS, NS), 0, 4) < 3).astype(jnp.int32), jax.random.fold_in(key_list[5], 1), 0, 1),
    }


def reference(wavefunction, left_env, right_env, coupling, left_shift, allowed):
    allowed_f = allowed.astype(jnp.float32)
    masked_psi = (wavefunction.astype(jnp.float32) * allowed_f[:, :, None, None]).astype(jnp.bfloat16)
    padded = jnp.pad(masked_psi, ((1, 1), (0, 0), (0, 0), (0, 0)))
    left_full = left_env.astype(jnp.float32)

    def per_right(column):
        psi_column = lax.dynamic_index_in_dim(padded, column, 1, keepdims=False)
        right_block = lax.dynamic_index_in_dim(right_env, column, 1, keepdims=False).astype(jnp.float32)
        factor = lax.dynamic_index_in_dim(coupling, column, 3, keepdims=False)
        keep_mask = lax.dynamic_index_in_dim(allowed_f, column, 1, keepdims=False)
        running = jnp.zeros((NW, NS, M, M), jnp.float32)
        for bond_index in range(LB):
            def pick_rows(moved_by):
                return lax.dynamic_slice_in_dim(psi_column, (moved_by + 1).astype(jnp.int32), NS, 0)

            sources = jax.vmap(pick_rows)(left_shift[:, bond_index]).astype(jnp.float32)
            product = jnp.einsum('waik,wakj->waij', left_full[:, bond_index], sources)
            running = running + product * factor[:, bond_index, :, None, None]
        partial_value = running.astype(jnp.bfloat16)
        combined = jnp.einsum('waij,wlj->ail', partial_value.astype(jnp.float32), right_block)
        return (combined * keep_mask[:, None, None]).astype(jnp.bfloat16)

    stacked = lax.map(per_right, jnp.arange(NS, dtype=jnp.int32))
    return jnp.transpose(stacked, (1, 0, 2, 3))
```

```python
import functools

import jax
import jax.numpy as jnp
from jax import lax
from jax.experimental import pallas as pl
from jax.experimental.pallas import tpu as pltpu
from jax.sharding import PartitionSpec as P

M = 128
LB = 5
NW = 8
G = 8
BOTH = ("sec", "term")
OFFSETS = (0, -1, 1, -2, 2, -3, 3, -4)
ROWS = LB * M
F32 = jnp.float32
BF16 = jnp.bfloat16
VMEM = pl.BlockSpec(memory_space=pltpu.VMEM)
SMEM = pl.BlockSpec(memory_space=pltpu.SMEM)
PARAMS = pltpu.CompilerParams(vmem_limit_bytes=24 * 1024 * 1024)


def together(*arrays):
    return lax.optimization_barrier(arrays)


def slot_bond(t, k):
    return lax.rem(t + OFFSETS[k] + NW, NW)


def left_products(factor_ref, shift_ref, *refs):
    envs, psi_ref, out_ref = refs[:NW], refs[NW], refs[NW + 1]
    for k in range(NW):
        rows = [shift_ref[k, c] + 1 for c in range(LB)]

        @pl.loop(0, G)
        def _(j):
            total = None
            for c in range(LB):
                product = jnp.dot(
                    envs[k][c * M : (c + 1) * M, :], psi_ref[rows[c], j], preferred_element_type=F32
                )
                product = product * factor_ref[k * LB + c, j]
                total = product if total is None else total + product
            out_ref[k, j] = total.astype(BF16)


def right_sum(t, j, i, partial_ref, right_ref, keep_ref):
    total = None
    for k in range(NW):
        product = lax.dot_general(
            partial_ref[k, j],
            right_ref[slot_bond(t, k) * (G // 2) + i],
            (((1,), (1,)), ((), ())),
            preferred_element_type=F32,
        )
        total = product if total is None else total + product
    return (total * keep_ref[0, j]).astype(BF16)


def right_own(where_ref, keep_ref, partial_ref, right_ref, out_ref):
    t, core = where_ref[0], where_ref[1]

    @pl.loop(0, G // 2)
    def _(i):
        out_ref[i] = right_sum(t, 2 * i + core, i, partial_ref, right_ref, keep_ref)


def right_other(where_ref, keep_ref, partial_ref, right_ref, own_ref, out_ref):
    t, core = where_ref[0], where_ref[1]

    @pl.loop(0, G // 2)
    def _(i):
        j = 2 * i + 1 - core
        value = right_sum(t, j, i, partial_ref, right_ref, keep_ref)
        out_ref[j] = value
        out_ref[G + j] = value
        mine = own_ref[i]
        out_ref[2 * i + core] = mine
        out_ref[G + 2 * i + core] = mine


def bf16_pieces(x):
    pieces = []
    for _ in range(3):
        piece = lax.reduce_precision(x, 8, 7)
        pieces.append(piece)
        x = x - piece
    return pieces


def on_device(wavefunction, left_env, right_env, coupling, left_shift, allowed, *, n_sec, n_term):
    s, t = lax.axis_index("sec"), lax.axis_index("term")
    groups = n_sec // G

    def device(sec, term):
        return sec * n_term + term

    spread = [(device(b, w), device(w * G + b % G, b // G)) for b in range(n_sec) for w in range(n_term)]
    by_core = [[2 * chip + core for chip in range(n_sec // 2)] for core in range(2)]
    up = [(i, (i + 1) % n_term) for i in range(n_term)]
    down = [(i, (i - 1) % n_term) for i in range(n_term)]
    exchange = [
        [device(A * G + i, B) for i in range(G)] + [device(B * G + i, A) for i in range(G)]
        for A in range(groups)
        for B in range(A + 1, groups)
    ] + [
        [device(A * G + i, A) for i in range(G)] + [device((A + 1) * G + i, A + 1) for i in range(G)]
        for A in range(0, groups, 2)
    ]

    right = lax.ppermute(right_env[0], BOTH, spread)

    row = lax.dynamic_slice_in_dim(coupling[0], s, 1, 1)[:, 0, :]
    table = jnp.concatenate(bf16_pieces(row) + [jnp.pad(left_shift.astype(F32), ((0, 0), (0, n_sec - LB)))])
    table = jnp.pad(table, ((0, 0), (0, M - n_sec))).astype(BF16)
    payload = jnp.concatenate([left_env[0, :, 0].reshape(ROWS, M), table])
    own_psi = lax.dynamic_slice_in_dim(wavefunction[0], t * G, G, 0)

    u1 = lax.ppermute(payload, "term", up)
    d1 = lax.ppermute(payload, "term", down)
    right, u1, d1 = together(right, u1, d1)
    halves = lax.all_to_all(
        jnp.tile(right, (n_sec // 2, 1, 1)), "sec", 0, 0, axis_index_groups=by_core, tiled=True
    )
    u2 = lax.ppermute(u1, "term", up)
    d2 = lax.ppermute(d1, "term", down)
    below = lax.ppermute(own_psi, "sec", [(i, i + 1) for i in range(n_sec - 1)])
    above = lax.ppermute(own_psi, "sec", [(i + 1, i) for i in range(n_sec - 1)])
    u2, d2 = together(u2, d2)
    u3 = lax.ppermute(u2, "term", up)
    d3 = lax.ppermute(d2, "term", down)
    u3, d3 = together(u3, d3)
    u4 = lax.ppermute(u3, "term", up)
    slots = [payload, u1, d1, u2, d2, u3, d3, u4]
    psi = jnp.stack([below, own_psi, above])

    tables = jnp.stack([x[ROWS:] for x in slots]).astype(F32)
    couplings = tables[:, :LB, :n_sec] + tables[:, LB : 2 * LB, :n_sec] + tables[:, 2 * LB : 3 * LB, :n_sec]
    couplings = lax.dynamic_slice_in_dim(couplings, t * G, G, 2)
    shifts = tables[:, 3 * LB, :LB].astype(jnp.int32)
    near = lax.dynamic_slice(jnp.pad(allowed, ((1, 1), (0, 0))), (s, t * G), (3, G)).astype(F32)
    source = shifts[:, :, None, None] + 1 == jnp.arange(3)[:, None]
    factors = couplings * jnp.sum(jnp.where(source, near, 0.0), axis=2)

    partial = pl.pallas_call(
        left_products,
        out_shape=jax.ShapeDtypeStruct((NW, G, M, M), BF16),
        in_specs=[SMEM, SMEM] + [VMEM] * (NW + 1),
        out_specs=VMEM,
        compiler_params=PARAMS,
        cost_estimate=pl.CostEstimate(flops=2 * 320 * M**3, bytes_accessed=5 << 20, transcendentals=0),
    )(factors.reshape(NW * LB, G), shifts, *slots, psi)

    halves, partial = together(halves, partial)
    others = lax.ppermute(halves, "sec", [(i, i ^ 1) for i in range(n_sec)])
    where = jnp.stack([t, lax.rem(s, 2)]).astype(jnp.int32)
    keep = lax.dynamic_slice(allowed, (s, t * G), (1, G)).astype(F32)
    cost = pl.CostEstimate(flops=2 * 32 * M**3, bytes_accessed=2 << 20, transcendentals=0)
    own = pl.pallas_call(
        right_own,
        out_shape=jax.ShapeDtypeStruct((G // 2, M, M), BF16),
        in_specs=[SMEM, SMEM, VMEM, VMEM],
        out_specs=VMEM,
        compiler_params=PARAMS,
        cost_estimate=cost,
    )(where, keep, partial, halves)
    results = pl.pallas_call(
        right_other,
        out_shape=jax.ShapeDtypeStruct((2 * G, M, M), BF16),
        in_specs=[SMEM, SMEM, VMEM, VMEM, VMEM],
        out_specs=VMEM,
        compiler_params=PARAMS,
        cost_estimate=cost,
    )(where, keep, partial, others, own)

    received = lax.all_to_all(results, BOTH, 0, 0, axis_index_groups=exchange, tiled=True)
    A = s // G
    first = jnp.where(A < t, G, jnp.where(A > t, 0, lax.rem(A, 2) * G))
    return lax.dynamic_slice_in_dim(received, first, G, 0)[:, None]


def solution(mesh):
    in_specs = (
        P("sec", None, None, None),
        P("term", None, "sec", None, None),
        P("term", "sec", None, None),
        P("term", None, None, None),
        P("term", None),
        P(),
    )
    body = functools.partial(on_device, n_sec=mesh.shape["sec"], n_term=mesh.shape["term"])
    return jax.shard_map(
        body, mesh=mesh, in_specs=in_specs, out_specs=P("term", "sec", None, None), check_vma=False
    )
```

```python
import functools

import jax
import jax.numpy as jnp
from jax import lax
from jax.experimental import pallas as pl
from jax.experimental.pallas import tpu as pltpu
from jax.sharding import PartitionSpec as P

M = 128
LB = 5
NW = 8
G = 8
BOTH = ("sec", "term")
OFFSETS = (0, -1, 1, -2, 2, -3, 3, -4)
ROWS = LB * M
F32 = jnp.float32
BF16 = jnp.bfloat16
VMEM = pl.BlockSpec(memory_space=pltpu.VMEM)
SMEM = pl.BlockSpec(memory_space=pltpu.SMEM)
PARAMS = pltpu.CompilerParams(vmem_limit_bytes=56 * 1024 * 1024)


def together(*arrays):
    return lax.optimization_barrier(arrays)


def slot_bond(t, k):
    return lax.rem(t + OFFSETS[k] + NW, NW)


def left_products(count, first, t_ref, *refs):
    slots = refs[:count]
    if first:
        below_ref, own_ref, above_ref, out_ref, psi_ref, factor_ref = refs[count:]
        for row, ref in enumerate((below_ref, own_ref, above_ref)):
            psi_ref[row] = ref[...]
    else:
        psi_ref, out_ref, factor_ref = refs[count:]
    sector = lax.broadcasted_iota(jnp.int32, (M, G * M), 0)
    wanted = lax.broadcasted_iota(jnp.int32, (M, G * M), 1) // M + t_ref[0] * G
    pick = jnp.where((sector == wanted) | (sector == wanted + M // 2), 1.0, 0.0).astype(BF16)
    for q, slot in enumerate(slots):
        table = slot[ROWS : ROWS + 16, :]
        spread = jnp.dot(table, pick, preferred_element_type=F32)
        factor_ref[q] = spread[:8] + spread[8:]
        shifts = table.astype(F32)[15:16, :]
        rows = [shifts[0, c].astype(jnp.int32) + 1 for c in range(LB)]
        envs = [slot[c * M : (c + 1) * M, :] for c in range(LB)]
        for start in range(0, G * M, 2 * M):
            totals = [None, None]
            for c in range(LB):
                product = lax.dot_general(
                    psi_ref[rows[c], start : start + 2 * M, :],
                    envs[c],
                    (((1,), (1,)), ((), ())),
                    preferred_element_type=F32,
                )
                for h in range(2):
                    at = start + h * M
                    term = product[h * M : (h + 1) * M] * factor_ref[q, c : c + 1, at : at + M]
                    totals[h] = term if totals[h] is None else totals[h] + term
            for h in range(2):
                at = start + h * M
                out_ref[q, at : at + M, :] = totals[h].astype(BF16)


def left_call(t, slots, psi, first):
    count = len(slots)
    out_shape = [jax.ShapeDtypeStruct((count, G * M, M), BF16)]
    if first:
        out_shape.append(jax.ShapeDtypeStruct((3, G * M, M), BF16))
    return pl.pallas_call(
        functools.partial(left_products, count, first),
        out_shape=out_shape,
        in_specs=[SMEM] + [VMEM] * (count + len(psi)),
        out_specs=[VMEM] * len(out_shape),
        scratch_shapes=[pltpu.VMEM((count, 8, G * M), F32)],
        compiler_params=PARAMS,
        cost_estimate=pl.CostEstimate(flops=2 * 40 * count * M**3, bytes_accessed=2 << 20, transcendentals=0),
    )(t, *slots, *psi)


def right_sum(t, j, i, partials, right_ref, keep_ref):
    total, k = None, 0
    for ref in partials:
        for q in range(ref.shape[0]):
            product = jnp.dot(
                right_ref[slot_bond(t, k) * (G // 2) + i],
                ref[q, pl.ds(pl.multiple_of(j * M, M), M), :],
                preferred_element_type=F32,
            )
            total = product if total is None else total + product
            k += 1
    return (total * keep_ref[0, j]).T.astype(BF16)


def right_own(where_ref, keep_ref, right_ref, *refs):
    partials, out_ref = refs[:-1], refs[-1]
    t, core = where_ref[0], where_ref[1]
    for i in range(G // 2):
        out_ref[i] = right_sum(t, 2 * i + core, i, partials, right_ref, keep_ref)


def right_other(where_ref, keep_ref, right_ref, own_ref, *refs):
    partials, out_ref = refs[:-1], refs[-1]
    t, core = where_ref[0], where_ref[1]
    for i in range(G // 2):
        j = 2 * i + 1 - core
        value = right_sum(t, j, i, partials, right_ref, keep_ref)
        out_ref[j] = value
        out_ref[G + j] = value
        mine = own_ref[i]
        out_ref[2 * i + core] = mine
        out_ref[G + 2 * i + core] = mine


def bf16_pieces(x):
    pieces = []
    for _ in range(3):
        piece = lax.reduce_precision(x, 8, 7)
        pieces.append(piece)
        x = x - piece
    return pieces


def on_device(wavefunction, left_env, right_env, coupling, left_shift, allowed, *, n_sec, n_term):
    s, t = lax.axis_index("sec"), lax.axis_index("term")
    groups = n_sec // G

    def device(sec, term):
        return sec * n_term + term

    spread = [(device(b, w), device(w * G + b % G, b // G)) for b in range(n_sec) for w in range(n_term)]
    by_core = [[2 * chip + core for chip in range(n_sec // 2)] for core in range(2)]
    up = [(i, (i + 1) % n_term) for i in range(n_term)]
    down = [(i, (i - 1) % n_term) for i in range(n_term)]
    exchange = [
        [device(A * G + i, B) for i in range(G)] + [device(B * G + i, A) for i in range(G)]
        for A in range(groups)
        for B in range(A + 1, groups)
    ] + [
        [device(A * G + i, A) for i in range(G)] + [device((A + 1) * G + i, A + 1) for i in range(G)]
        for A in range(0, groups, 2)
    ]

    right = lax.ppermute(right_env[0], BOTH, spread)

    near = lax.dynamic_slice_in_dim(jnp.pad(allowed, ((1, 1), (0, 0))), s, 3, 0)
    source = left_shift[0, :, None] + 1 == jnp.arange(3)
    kept = jnp.sum(jnp.where(source[:, :, None], near, 0), axis=1)
    factors = lax.dynamic_slice_in_dim(coupling[0], s, 1, 1)[:, 0, :] * kept.astype(F32)
    high, middle, low = bf16_pieces(factors)
    table = jnp.concatenate(
        [
            jnp.pad(jnp.concatenate([high, middle], axis=1), ((0, 8 - LB), (0, 0))),
            jnp.pad(low, ((0, 7 - LB), (0, M - n_sec))),
            jnp.pad(left_shift.astype(F32), ((0, 0), (0, M - LB))),
        ]
    ).astype(BF16)
    payload = jnp.concatenate([left_env[0, :, 0].reshape(ROWS, M), table])
    own_psi = lax.dynamic_slice_in_dim(wavefunction[0], t * G, G, 0)
    own_psi = jnp.swapaxes(own_psi, 1, 2).reshape(G * M, M)
    here = t.astype(jnp.int32)[None]

    u1 = lax.ppermute(payload, "term", up)
    d1 = lax.ppermute(payload, "term", down)
    right, own_psi = together(right, own_psi)
    below = lax.ppermute(own_psi, "sec", [(i, i + 1) for i in range(n_sec - 1)])
    above = lax.ppermute(own_psi, "sec", [(i + 1, i) for i in range(n_sec - 1)])
    right, u1, d1 = together(right, u1, d1)
    halves = lax.all_to_all(
        jnp.tile(right, (n_sec // 2, 1, 1)), "sec", 0, 0, axis_index_groups=by_core, tiled=True
    )
    u2 = lax.ppermute(u1, "term", up)
    d2 = lax.ppermute(d1, "term", down)
    part0, psi = left_call(here, [payload], [below, own_psi, above], True)
    (part1,) = left_call(here, [u1, d1], [psi], False)
    u2, d2, part1 = together(u2, d2, part1)
    u3 = lax.ppermute(u2, "term", up)
    d3 = lax.ppermute(d2, "term", down)
    (part2,) = left_call(here, [u2, d2], [psi], False)
    u3, d3, part2 = together(u3, d3, part2)
    u4 = lax.ppermute(u3, "term", up)
    (part3,) = left_call(here, [u3, d3], [psi], False)
    u4, part3 = together(u4, part3)
    (part4,) = left_call(here, [u4], [psi], False)
    parts = [part0, part1, part2, part3, part4]

    halves, parts[-1] = together(halves, parts[-1])
    others = lax.ppermute(halves, "sec", [(i, i ^ 1) for i in range(n_sec)])
    where = jnp.stack([t, lax.rem(s, 2)]).astype(jnp.int32)
    keep = lax.dynamic_slice(allowed, (s, t * G), (1, G)).astype(F32)
    cost = pl.CostEstimate(flops=2 * 32 * M**3, bytes_accessed=2 << 20, transcendentals=0)
    own = pl.pallas_call(
        right_own,
        out_shape=jax.ShapeDtypeStruct((G // 2, M, M), BF16),
        in_specs=[SMEM, SMEM] + [VMEM] * (1 + len(parts)),
        out_specs=VMEM,
        compiler_params=PARAMS,
        cost_estimate=cost,
    )(where, keep, halves, *parts)
    results = pl.pallas_call(
        right_other,
        out_shape=jax.ShapeDtypeStruct((2 * G, M, M), BF16),
        in_specs=[SMEM, SMEM] + [VMEM] * (2 + len(parts)),
        out_specs=VMEM,
        compiler_params=PARAMS,
        cost_estimate=cost,
    )(where, keep, others, own, *parts)

    received = lax.all_to_all(results, BOTH, 0, 0, axis_index_groups=exchange, tiled=True)
    A = s // G
    first = jnp.where(A < t, G, jnp.where(A > t, 0, lax.rem(A, 2) * G))
    return lax.dynamic_slice_in_dim(received, first, G, 0)[:, None]


def solution(mesh):
    in_specs = (
        P("sec", None, None, None),
        P("term", None, "sec", None, None),
        P("term", "sec", None, None),
        P("term", None, None, None),
        P("term", None),
        P(),
    )
    body = functools.partial(on_device, n_sec=mesh.shape["sec"], n_term=mesh.shape["term"])
    return jax.shard_map(
        body, mesh=mesh, in_specs=in_specs, out_specs=P("term", "sec", None, None), check_vma=False
    )
```

```python
import functools

import jax
import jax.numpy as jnp
from jax import lax
from jax.experimental import pallas as pl
from jax.experimental.pallas import tpu as pltpu
from jax.sharding import PartitionSpec as P

M = 128
LB = 5
NW = 8
G = 8
BOTH = ("sec", "term")
ROWS = LB * M
F32 = jnp.float32
BF16 = jnp.bfloat16
VMEM = pl.BlockSpec(memory_space=pltpu.VMEM)
SMEM = pl.BlockSpec(memory_space=pltpu.SMEM)
PARAMS = pltpu.CompilerParams(vmem_limit_bytes=56 * 1024 * 1024)


def together(*arrays):
    return lax.optimization_barrier(arrays)


def prepare(place_ref, shift_ref, psi_ref, env_ref, coupling_ref, allowed_ref, payload_ref, turned_ref, table_ref):
    for j in range(G):
        turned_ref[j * M : (j + 1) * M, :] = psi_ref[0, j].T
    s = place_ref[0]
    n_sec = allowed_ref.shape[0]
    payload_ref[:ROWS, :] = env_ref[...]
    table_ref[...] = jnp.zeros_like(table_ref)
    lane = lax.broadcasted_iota(jnp.int32, (1, M), 1)
    shifts = jnp.zeros((1, M), F32)
    for c in range(LB):
        shift = shift_ref[0, c]
        source = s + shift
        inside = jnp.logical_and(source >= 0, source < n_sec).astype(F32)
        kept = allowed_ref[pl.ds(jnp.clip(source, 0, n_sec - 1), 1), :].astype(F32) * inside
        factor = coupling_ref[c, pl.ds(s, 1), :] * kept
        high = factor.astype(BF16).astype(F32)
        middle = (factor - high).astype(BF16).astype(F32)
        low = (factor - high - middle).astype(BF16).astype(F32)
        table_ref[c : c + 1, :] = jnp.concatenate([high, middle], axis=1)
        table_ref[8 + c : 9 + c, :n_sec] = low
        shifts = jnp.where(lane == c, shift.astype(F32), shifts)
    table_ref[15:16, :] = shifts
    payload_ref[ROWS:, :] = table_ref[...].astype(BF16)


def left_products(t_ref, slots, below_ref, own_ref, above_ref, out_ref, psi_ref, factor_ref):
    for row, ref in enumerate((below_ref, own_ref, above_ref)):
        psi_ref[row] = ref[...]
    sector = lax.broadcasted_iota(jnp.int32, (M, G * M), 0)
    wanted = lax.broadcasted_iota(jnp.int32, (M, G * M), 1) // M + t_ref[0] * G
    pick = jnp.where((sector == wanted) | (sector == wanted + M // 2), 1.0, 0.0).astype(BF16)

    @pl.loop(0, NW)
    def _(w):
        table = slots[w, ROWS : ROWS + 16, :]
        spread = jnp.dot(table, pick, preferred_element_type=F32)
        factor_ref[...] = spread[:8] + spread[8:]
        shifts = table.astype(F32)[15:16, :]
        rows = [shifts[0, c].astype(jnp.int32) + 1 for c in range(LB)]
        envs = [slots[w, c * M : (c + 1) * M, :] for c in range(LB)]
        for start in range(0, G * M, 2 * M):
            totals = [None, None]
            for c in range(LB):
                product = lax.dot_general(
                    psi_ref[rows[c], start : start + 2 * M, :],
                    envs[c],
                    (((1,), (1,)), ((), ())),
                    preferred_element_type=F32,
                )
                for h in range(2):
                    at = start + h * M
                    term = product[h * M : (h + 1) * M] * factor_ref[c : c + 1, at : at + M]
                    totals[h] = term if totals[h] is None else totals[h] + term
            for h in range(2):
                at = start + h * M
                out_ref[w, at : at + M, :] = totals[h].astype(BF16)


def right_sum(j, i, partial_ref, right_ref, keep_ref):
    total = None
    for w in range(NW):
        product = jnp.dot(
            right_ref[w * (G // 2) + i],
            partial_ref[w, pl.ds(pl.multiple_of(j * M, M), M), :],
            preferred_element_type=F32,
        )
        total = product if total is None else total + product
    return (total * keep_ref[0, j]).T.astype(BF16)


def right_own(core_ref, keep_ref, right_ref, partial_ref, out_ref):
    core = core_ref[0]
    for i in range(G // 2):
        out_ref[i] = right_sum(2 * i + core, i, partial_ref, right_ref, keep_ref)


def right_other(core_ref, keep_ref, right_ref, own_ref, partial_ref, out_ref):
    core = core_ref[0]
    for i in range(G // 2):
        j = 2 * i + 1 - core
        value = right_sum(j, i, partial_ref, right_ref, keep_ref)
        out_ref[j] = value
        out_ref[G + j] = value
        mine = own_ref[i]
        out_ref[2 * i + core] = mine
        out_ref[G + 2 * i + core] = mine


def on_device(wavefunction, left_env, right_env, coupling, left_shift, allowed, *, n_sec, n_term):
    s, t = lax.axis_index("sec"), lax.axis_index("term")
    groups = n_sec // G

    def device(sec, term):
        return sec * n_term + term

    spread = [(device(b, w), device(w * G + b % G, b // G)) for b in range(n_sec) for w in range(n_term)]
    by_core = [[2 * chip + core for chip in range(n_sec // 2)] for core in range(2)]
    exchange = [
        [device(A * G + i, B) for i in range(G)] + [device(B * G + i, A) for i in range(G)]
        for A in range(groups)
        for B in range(A + 1, groups)
    ] + [
        [device(A * G + i, A) for i in range(G)] + [device((A + 1) * G + i, A + 1) for i in range(G)]
        for A in range(0, groups, 2)
    ]

    right = lax.ppermute(right_env[0], BOTH, spread)

    place = jnp.stack([s, t]).astype(jnp.int32)
    payload, own_psi = pl.pallas_call(
        prepare,
        grid_spec=pltpu.PrefetchScalarGridSpec(
            num_scalar_prefetch=2,
            grid=(1,),
            in_specs=[
                pl.BlockSpec((1, G, M, M), lambda i, place, shift: (0, place[1], 0, 0)),
                pl.BlockSpec((ROWS, M), lambda i, place, shift: (0, 0)),
                pl.BlockSpec(coupling.shape[1:], lambda i, place, shift: (0, 0, 0)),
                pl.BlockSpec(allowed.shape, lambda i, place, shift: (0, 0)),
            ],
            out_specs=[
                pl.BlockSpec((ROWS + 16, M), lambda i, place, shift: (0, 0)),
                pl.BlockSpec((G * M, M), lambda i, place, shift: (0, 0)),
            ],
            scratch_shapes=[pltpu.VMEM((16, M), F32)],
        ),
        out_shape=[jax.ShapeDtypeStruct((ROWS + 16, M), BF16), jax.ShapeDtypeStruct((G * M, M), BF16)],
        compiler_params=PARAMS,
    )(place, left_shift, wavefunction, left_env.reshape(ROWS, M), coupling[0], allowed)
    here = t.astype(jnp.int32)[None]

    payloads = lax.all_gather(payload, "term")
    below = lax.ppermute(own_psi, "sec", [(i, i + 1) for i in range(n_sec - 1)])
    above = lax.ppermute(own_psi, "sec", [(i + 1, i) for i in range(n_sec - 1)])
    right, below, above = together(right, below, above)
    halves = lax.all_to_all(
        jnp.tile(right, (n_sec // 2, 1, 1)), "sec", 0, 0, axis_index_groups=by_core, tiled=True
    )
    partial = pl.pallas_call(
        left_products,
        out_shape=jax.ShapeDtypeStruct((NW, G * M, M), BF16),
        in_specs=[SMEM] + [VMEM] * 4,
        out_specs=VMEM,
        scratch_shapes=[pltpu.VMEM((3, G * M, M), BF16), pltpu.VMEM((8, G * M), F32)],
        compiler_params=PARAMS,
        cost_estimate=pl.CostEstimate(flops=2 * 320 * M**3, bytes_accessed=5 << 20, transcendentals=0),
    )(here, payloads, below, own_psi, above)

    halves, partial = together(halves, partial)
    others = lax.ppermute(halves, "sec", [(i, i ^ 1) for i in range(n_sec)])
    core = lax.rem(s, 2).astype(jnp.int32)[None]
    keep = lax.dynamic_slice(allowed, (s, t * G), (1, G)).astype(F32)
    cost = pl.CostEstimate(flops=2 * 32 * M**3, bytes_accessed=2 << 20, transcendentals=0)
    own = pl.pallas_call(
        right_own,
        out_shape=jax.ShapeDtypeStruct((G // 2, M, M), BF16),
        in_specs=[SMEM, SMEM] + [VMEM] * 2,
        out_specs=VMEM,
        compiler_params=PARAMS,
        cost_estimate=cost,
    )(core, keep, halves, partial)
    results = pl.pallas_call(
        right_other,
        out_shape=jax.ShapeDtypeStruct((2 * G, M, M), BF16),
        in_specs=[SMEM, SMEM] + [VMEM] * 3,
        out_specs=VMEM,
        compiler_params=PARAMS,
        cost_estimate=cost,
    )(core, keep, others, own, partial)

    received = lax.all_to_all(results, BOTH, 0, 0, axis_index_groups=exchange, tiled=True)
    A = s // G
    first = jnp.where(A < t, G, jnp.where(A > t, 0, lax.rem(A, 2) * G))
    return lax.dynamic_slice_in_dim(received, first, G, 0)[:, None]


def solution(mesh):
    in_specs = (
        P("sec", None, None, None),
        P("term", None, "sec", None, None),
        P("term", "sec", None, None),
        P("term", None, None, None),
        P("term", None),
        P(),
    )
    body = functools.partial(on_device, n_sec=mesh.shape["sec"], n_term=mesh.shape["term"])
    return jax.shard_map(
        body, mesh=mesh, in_specs=in_specs, out_specs=P("term", "sec", None, None), check_vma=False
    )
```

```python
import functools

import jax
import jax.numpy as jnp
from jax import lax
from jax.experimental import pallas as pl
from jax.experimental.pallas import tpu as pltpu
from jax.sharding import PartitionSpec as P

M = 128
LB = 5
NW = 8
G = 8
BOTH = ("sec", "term")
ROWS = LB * M
F32 = jnp.float32
BF16 = jnp.bfloat16
VMEM = pl.BlockSpec(memory_space=pltpu.VMEM)
SMEM = pl.BlockSpec(memory_space=pltpu.SMEM)
PARAMS = pltpu.CompilerParams(vmem_limit_bytes=56 * 1024 * 1024)


def together(*arrays):
    return lax.optimization_barrier(arrays)


def prepare(place_ref, shift_ref, psi_ref, env_ref, coupling_ref, allowed_ref, payload_ref, turned_ref, table_ref):
    for j in range(G):
        turned_ref[j * M : (j + 1) * M, :] = psi_ref[0, j].T
    s = place_ref[0]
    n_sec = allowed_ref.shape[0]
    payload_ref[:ROWS, :] = env_ref[...]
    table_ref[...] = jnp.zeros_like(table_ref)
    lane = lax.broadcasted_iota(jnp.int32, (1, M), 1)
    shifts = jnp.zeros((1, M), F32)
    for c in range(LB):
        shift = shift_ref[0, c]
        source = s + shift
        inside = jnp.logical_and(source >= 0, source < n_sec).astype(F32)
        kept = allowed_ref[pl.ds(jnp.clip(source, 0, n_sec - 1), 1), :].astype(F32) * inside
        factor = coupling_ref[c, pl.ds(s, 1), :] * kept
        high = factor.astype(BF16).astype(F32)
        middle = (factor - high).astype(BF16).astype(F32)
        low = (factor - high - middle).astype(BF16).astype(F32)
        table_ref[c : c + 1, :] = jnp.concatenate([high, middle], axis=1)
        table_ref[8 + c : 9 + c, :n_sec] = low
        shifts = jnp.where(lane == c, shift.astype(F32), shifts)
    table_ref[15:16, :] = shifts
    payload_ref[ROWS:, :] = table_ref[...].astype(BF16)


def left_products(t_ref, slots, below_ref, own_ref, above_ref, out_ref, psi_ref, factor_ref):
    for row, ref in enumerate((below_ref, own_ref, above_ref)):
        psi_ref[row] = ref[...]
    sector = lax.broadcasted_iota(jnp.int32, (M, G * M), 0)
    wanted = lax.broadcasted_iota(jnp.int32, (M, G * M), 1) // M + t_ref[0] * G
    pick = jnp.where((sector == wanted) | (sector == wanted + M // 2), 1.0, 0.0).astype(BF16)

    @pl.loop(0, NW)
    def _(w):
        table = slots[w, ROWS : ROWS + 16, :]
        spread = jnp.dot(table, pick, preferred_element_type=F32)
        factor_ref[...] = spread[:8] + spread[8:]
        shifts = table.astype(F32)[15:16, :]
        rows = [shifts[0, c].astype(jnp.int32) + 1 for c in range(LB)]
        envs = [slots[w, c * M : (c + 1) * M, :] for c in range(LB)]
        for start in range(0, G * M, 2 * M):
            totals = [None, None]
            for c in range(LB):
                product = lax.dot_general(
                    psi_ref[rows[c], start : start + 2 * M, :],
                    envs[c],
                    (((1,), (1,)), ((), ())),
                    preferred_element_type=F32,
                )
                for h in range(2):
                    at = start + h * M
                    term = product[h * M : (h + 1) * M] * factor_ref[c : c + 1, at : at + M]
                    totals[h] = term if totals[h] is None else totals[h] + term
            for h in range(2):
                out_ref[start // M + h, pl.ds(pl.multiple_of(w * M, M), M), :] = totals[h].astype(BF16)


def right_sum(j, i, partial_ref, right_ref, keep_ref):
    right = jnp.concatenate([right_ref[w * (G // 2) + i] for w in range(NW)], axis=1)
    total = jnp.dot(right, partial_ref[j], preferred_element_type=F32)
    return (total * keep_ref[0, j]).T.astype(BF16)


def right_own(core_ref, keep_ref, right_ref, partial_ref, out_ref):
    core = core_ref[0]
    for i in range(G // 2):
        out_ref[i] = right_sum(2 * i + core, i, partial_ref, right_ref, keep_ref)


def right_other(core_ref, keep_ref, right_ref, own_ref, partial_ref, out_ref):
    core = core_ref[0]
    for i in range(G // 2):
        j = 2 * i + 1 - core
        value = right_sum(j, i, partial_ref, right_ref, keep_ref)
        out_ref[j] = value
        out_ref[G + j] = value
        mine = own_ref[i]
        out_ref[2 * i + core] = mine
        out_ref[G + 2 * i + core] = mine


def on_device(wavefunction, left_env, right_env, coupling, left_shift, allowed, *, n_sec, n_term):
    s, t = lax.axis_index("sec"), lax.axis_index("term")
    groups = n_sec // G

    def device(sec, term):
        return sec * n_term + term

    spread = [(device(b, w), device(w * G + b % G, b // G)) for b in range(n_sec) for w in range(n_term)]
    by_core = [[2 * chip + core for chip in range(n_sec // 2)] for core in range(2)]
    exchange = [
        [device(A * G + i, B) for i in range(G)] + [device(B * G + i, A) for i in range(G)]
        for A in range(groups)
        for B in range(A + 1, groups)
    ] + [
        [device(A * G + i, A) for i in range(G)] + [device((A + 1) * G + i, A + 1) for i in range(G)]
        for A in range(0, groups, 2)
    ]

    right = lax.ppermute(right_env[0], BOTH, spread)

    place = jnp.stack([s, t]).astype(jnp.int32)
    payload, own_psi = pl.pallas_call(
        prepare,
        grid_spec=pltpu.PrefetchScalarGridSpec(
            num_scalar_prefetch=2,
            grid=(1,),
            in_specs=[
                pl.BlockSpec((1, G, M, M), lambda i, place, shift: (0, place[1], 0, 0)),
                pl.BlockSpec((ROWS, M), lambda i, place, shift: (0, 0)),
                pl.BlockSpec(coupling.shape[1:], lambda i, place, shift: (0, 0, 0)),
                pl.BlockSpec(allowed.shape, lambda i, place, shift: (0, 0)),
            ],
            out_specs=[
                pl.BlockSpec((ROWS + 16, M), lambda i, place, shift: (0, 0)),
                pl.BlockSpec((G * M, M), lambda i, place, shift: (0, 0)),
            ],
            scratch_shapes=[pltpu.VMEM((16, M), F32)],
        ),
        out_shape=[jax.ShapeDtypeStruct((ROWS + 16, M), BF16), jax.ShapeDtypeStruct((G * M, M), BF16)],
        compiler_params=PARAMS,
    )(place, left_shift, wavefunction, left_env.reshape(ROWS, M), coupling[0], allowed)
    here = t.astype(jnp.int32)[None]

    payloads = lax.all_gather(payload, "term")
    right, own_psi = together(right, own_psi)
    below = lax.ppermute(own_psi, "sec", [(i, i + 1) for i in range(n_sec - 1)])
    above = lax.ppermute(own_psi, "sec", [(i + 1, i) for i in range(n_sec - 1)])
    halves = lax.all_to_all(
        jnp.tile(right, (n_sec // 2, 1, 1)), "sec", 0, 0, axis_index_groups=by_core, tiled=True
    )
    partial = pl.pallas_call(
        left_products,
        out_shape=jax.ShapeDtypeStruct((G, NW * M, M), BF16),
        in_specs=[SMEM] + [VMEM] * 4,
        out_specs=VMEM,
        scratch_shapes=[pltpu.VMEM((3, G * M, M), BF16), pltpu.VMEM((8, G * M), F32)],
        compiler_params=PARAMS,
        cost_estimate=pl.CostEstimate(flops=2 * 320 * M**3, bytes_accessed=5 << 20, transcendentals=0),
    )(here, payloads, below, own_psi, above)

    halves, partial = together(halves, partial)
    others = lax.ppermute(halves, "sec", [(i, i ^ 1) for i in range(n_sec)])
    core = lax.rem(s, 2).astype(jnp.int32)[None]
    keep = lax.dynamic_slice(allowed, (s, t * G), (1, G)).astype(F32)
    cost = pl.CostEstimate(flops=2 * 32 * M**3, bytes_accessed=2 << 20, transcendentals=0)
    own = pl.pallas_call(
        right_own,
        out_shape=jax.ShapeDtypeStruct((G // 2, M, M), BF16),
        in_specs=[SMEM, SMEM] + [VMEM] * 2,
        out_specs=VMEM,
        compiler_params=PARAMS,
        cost_estimate=cost,
    )(core, keep, halves, partial)
    results = pl.pallas_call(
        right_other,
        out_shape=jax.ShapeDtypeStruct((2 * G, M, M), BF16),
        in_specs=[SMEM, SMEM] + [VMEM] * 3,
        out_specs=VMEM,
        compiler_params=PARAMS,
        cost_estimate=cost,
    )(core, keep, others, own, partial)

    received = lax.all_to_all(results, BOTH, 0, 0, axis_index_groups=exchange, tiled=True)
    A = s // G
    first = jnp.where(A < t, G, jnp.where(A > t, 0, lax.rem(A, 2) * G))
    return lax.dynamic_slice_in_dim(received, first, G, 0)[:, None]


def solution(mesh):
    in_specs = (
        P("sec", None, None, None),
        P("term", None, "sec", None, None),
        P("term", "sec", None, None),
        P("term", None, None, None),
        P("term", None),
        P(),
    )
    body = functools.partial(on_device, n_sec=mesh.shape["sec"], n_term=mesh.shape["term"])
    return jax.shard_map(
        body, mesh=mesh, in_specs=in_specs, out_specs=P("term", "sec", None, None), check_vma=False
    )
```

```python
import functools

import jax
import jax.numpy as jnp
from jax import lax
from jax.experimental import pallas as pl
from jax.experimental.pallas import tpu as pltpu
from jax.sharding import PartitionSpec as P

M = 128
LB = 5
NW = 8
G = 8
H = G // 2
BOTH = ("sec", "term")
ROWS = LB * M
F32 = jnp.float32
BF16 = jnp.bfloat16
VMEM = pl.BlockSpec(memory_space=pltpu.VMEM)
SMEM = pl.BlockSpec(memory_space=pltpu.SMEM)
PARAMS = pltpu.CompilerParams(vmem_limit_bytes=56 * 1024 * 1024)


def together(*arrays):
    return lax.optimization_barrier(arrays)


def right_chip(t, w, i):
    return w // 2 * G + (t % 2 * H + 2 * i + w % 2 + G - 2) % G


def prepare(place_ref, shift_ref, psi_ref, env_ref, coupling_ref, allowed_ref, payload_ref, turned_ref, table_ref):
    s = place_ref[0]
    core = lax.rem(s, 2)
    for i in range(H):
        turned_ref[i * M : (i + 1) * M, :] = psi_ref[0, 2 * i + core].T
        turned_ref[(H + i) * M : (H + i + 1) * M, :] = psi_ref[0, 2 * i + 1 - core].T
    n_sec = allowed_ref.shape[0]
    payload_ref[:ROWS, :] = env_ref[...]
    table_ref[...] = jnp.zeros_like(table_ref)
    lane = lax.broadcasted_iota(jnp.int32, (1, M), 1)
    shifts = jnp.zeros((1, M), F32)
    for c in range(LB):
        shift = shift_ref[0, c]
        source = s + shift
        inside = jnp.logical_and(source >= 0, source < n_sec).astype(F32)
        kept = allowed_ref[pl.ds(jnp.clip(source, 0, n_sec - 1), 1), :].astype(F32) * inside
        factor = coupling_ref[c, pl.ds(s, 1), :] * kept
        high = factor.astype(BF16).astype(F32)
        middle = (factor - high).astype(BF16).astype(F32)
        low = (factor - high - middle).astype(BF16).astype(F32)
        table_ref[c : c + 1, :] = jnp.concatenate([high, middle], axis=1)
        table_ref[8 + c : 9 + c, :n_sec] = low
        shifts = jnp.where(lane == c, shift.astype(F32), shifts)
    table_ref[15:16, :] = shifts
    payload_ref[ROWS:, :] = table_ref[...].astype(BF16)


def left_products(first_row, place_ref, slots, *refs):
    near_ref, turned_ref, inner_ref, far_ref, out_ref, psi_ref, factor_ref = refs
    psi_ref[0] = near_ref[H * M :, :]
    psi_ref[1] = turned_ref[: H * M, :]
    psi_ref[2] = inner_ref[...]
    psi_ref[3] = far_ref[...]
    s, t = place_ref[0], place_ref[1]
    core = lax.rem(s, 2)
    sector = lax.broadcasted_iota(jnp.int32, (M, H * M), 0)
    wanted = lax.broadcasted_iota(jnp.int32, (M, H * M), 1) // M * 2 + t * G + core
    pick = jnp.where((sector == wanted) | (sector == wanted + M // 2), 1.0, 0.0).astype(BF16)

    @pl.loop(0, NW)
    def _(w):
        table = slots[w, ROWS : ROWS + 16, :]
        spread = jnp.dot(table, pick, preferred_element_type=F32)
        factor_ref[...] = spread[:8] + spread[8:]
        shifts = table.astype(F32)[15:16, :]
        rows = [first_row + shifts[0, c].astype(jnp.int32) * (1 - 2 * core) for c in range(LB)]
        envs = [slots[w, c * M : (c + 1) * M, :] for c in range(LB)]
        for start in range(0, H * M, 2 * M):
            totals = [None, None]
            for c in range(LB):
                product = lax.dot_general(
                    psi_ref[rows[c], start : start + 2 * M, :],
                    envs[c],
                    (((1,), (1,)), ((), ())),
                    preferred_element_type=F32,
                )
                for h in range(2):
                    at = start + h * M
                    term = product[h * M : (h + 1) * M] * factor_ref[c : c + 1, at : at + M]
                    totals[h] = term if totals[h] is None else totals[h] + term
            for h in range(2):
                out_ref[start // M + h, pl.ds(pl.multiple_of(w * M, M), M), :] = totals[h].astype(BF16)


def right_products(place_ref, allowed_ref, right_ref, own_ref, other_ref, out_ref):
    s, t = place_ref[0], place_ref[1]
    core = lax.rem(s, 2)
    for i in range(H):
        right = jnp.concatenate([right_ref[right_chip(t, w, i)] for w in range(NW)], axis=1)
        for partial_ref, which in ((own_ref, core), (other_ref, 1 - core)):
            total = jnp.dot(right, partial_ref[i], preferred_element_type=F32)
            keep = allowed_ref[s - core + which, t * G + 2 * i + core].astype(F32)
            value = (total * keep).T.astype(BF16)
            out_ref[i, which] = value
            out_ref[H + i, which] = value


def on_device(wavefunction, left_env, right_env, coupling, left_shift, allowed, *, n_sec, n_term):
    s, t = lax.axis_index("sec"), lax.axis_index("term")
    groups = n_sec // G

    def device(sec, term):
        return sec * n_term + term

    spread = [
        (device(b, w), device(2 * right_chip(b // G, w, b % G // 2) + b % 2, b // G))
        for b in range(n_sec)
        for w in range(n_term)
    ]
    by_core = [[2 * chip + core for chip in range(n_sec // 2)] for core in range(2)]
    exchange = []
    for core in range(2):

        def members(A, B):
            return [device(A * G + 2 * i + core, B) for i in range(H)]

        exchange += [members(A, B) + members(B, A) for A in range(groups) for B in range(A + 1, groups)]
        exchange += [members(A, A) + members(A + 1, A + 1) for A in range(0, groups, 2)]

    right = lax.ppermute(right_env[0], BOTH, spread)
    place = jnp.stack([s, t]).astype(jnp.int32)
    payload, turned = pl.pallas_call(
        prepare,
        grid_spec=pltpu.PrefetchScalarGridSpec(
            num_scalar_prefetch=2,
            grid=(1,),
            in_specs=[
                pl.BlockSpec((1, G, M, M), lambda i, place, shift: (0, place[1], 0, 0)),
                pl.BlockSpec((ROWS, M), lambda i, place, shift: (0, 0)),
                pl.BlockSpec(coupling.shape[1:], lambda i, place, shift: (0, 0, 0)),
                pl.BlockSpec(allowed.shape, lambda i, place, shift: (0, 0)),
            ],
            out_specs=[
                pl.BlockSpec((ROWS + 16, M), lambda i, place, shift: (0, 0)),
                pl.BlockSpec((G * M, M), lambda i, place, shift: (0, 0)),
            ],
            scratch_shapes=[pltpu.VMEM((16, M), F32)],
        ),
        out_shape=[jax.ShapeDtypeStruct((ROWS + 16, M), BF16), jax.ShapeDtypeStruct((G * M, M), BF16)],
        compiler_params=PARAMS,
    )(place, left_shift, wavefunction, left_env.reshape(ROWS, M), coupling[0], allowed)

    payloads = lax.all_gather(payload, "term")
    across = [(i, i ^ 1) for i in range(n_sec)]
    near = lax.ppermute(turned, "sec", [(i, i + 1) if i % 2 else (i, i - 1) for i in range(1, n_sec - 1)])
    right, near = together(right, near)
    inner = lax.ppermute(turned[H * M :], "sec", across)
    far = lax.ppermute(near[: H * M], "sec", across)
    right = lax.all_to_all(
        jnp.tile(right, (n_sec // 2, 1, 1)), "sec", 0, 0, axis_index_groups=by_core, tiled=True
    )
    payloads, inner, far = together(payloads, inner, far)
    other_payloads = lax.ppermute(payloads, "sec", across)

    def left_call(first_row, slots):
        return pl.pallas_call(
            functools.partial(left_products, first_row),
            out_shape=jax.ShapeDtypeStruct((H, NW * M, M), BF16),
            in_specs=[SMEM] + [VMEM] * 5,
            out_specs=VMEM,
            scratch_shapes=[pltpu.VMEM((4, H * M, M), BF16), pltpu.VMEM((8, H * M), F32)],
            compiler_params=PARAMS,
            cost_estimate=pl.CostEstimate(flops=2 * 160 * M**3, bytes_accessed=3 << 20, transcendentals=0),
        )(place, slots, near, turned, inner, far)

    own = left_call(1, payloads)
    other = left_call(2, other_payloads)
    right, other = together(right, other)
    results = pl.pallas_call(
        right_products,
        out_shape=jax.ShapeDtypeStruct((G, 2, M, M), BF16),
        in_specs=[SMEM, SMEM] + [VMEM] * 3,
        out_specs=VMEM,
        compiler_params=PARAMS,
        cost_estimate=pl.CostEstimate(flops=2 * 64 * M**3, bytes_accessed=4 << 20, transcendentals=0),
    )(place, allowed, right, own, other)

    received = lax.all_to_all(results, BOTH, 0, 0, axis_index_groups=exchange, tiled=True)
    A = s // G
    first = jnp.where(A < t, H, jnp.where(A > t, 0, lax.rem(A, 2) * H))
    return lax.dynamic_slice_in_dim(received, first, H, 0).reshape(G, 1, M, M)


def solution(mesh):
    in_specs = (
        P("sec", None, None, None),
        P("term", None, "sec", None, None),
        P("term", "sec", None, None),
        P("term", None, None, None),
        P("term", None),
        P(),
    )
    body = functools.partial(on_device, n_sec=mesh.shape["sec"], n_term=mesh.shape["term"])
    return jax.shard_map(
        body, mesh=mesh, in_specs=in_specs, out_specs=P("term", "sec", None, None), check_vma=False
    )
```

```python
import functools

import jax
import jax.numpy as jnp
from jax import lax
from jax.experimental import pallas as pl
from jax.experimental.pallas import tpu as pltpu
from jax.sharding import PartitionSpec as P

M = 128
LB = 5
NW = 8
G = 8
H = G // 2
BOTH = ("sec", "term")
ROWS = LB * M
F32 = jnp.float32
BF16 = jnp.bfloat16
VMEM = pl.BlockSpec(memory_space=pltpu.VMEM)
SMEM = pl.BlockSpec(memory_space=pltpu.SMEM)
PARAMS = pltpu.CompilerParams(vmem_limit_bytes=56 * 1024 * 1024)


def together(*arrays):
    return lax.optimization_barrier(arrays)


def right_chip(t, w, i):
    return w // 2 * G + (t % 2 * H + 2 * i + w % 2 + G - 2) % G


def pack(shift_ref, env_ref, coupling_ref, allowed_ref, payload_ref, table_ref):
    s = lax.axis_index("sec")
    n_sec = allowed_ref.shape[0]
    payload_ref[:ROWS, :] = env_ref[...]
    table_ref[...] = jnp.zeros_like(table_ref)
    lane = lax.broadcasted_iota(jnp.int32, (1, M), 1)
    shifts = jnp.zeros((1, M), F32)
    for c in range(LB):
        shift = shift_ref[0, c]
        source = s + shift
        inside = jnp.logical_and(source >= 0, source < n_sec).astype(F32)
        kept = allowed_ref[pl.ds(jnp.clip(source, 0, n_sec - 1), 1), :].astype(F32) * inside
        factor = coupling_ref[c, pl.ds(s, 1), :] * kept
        high = factor.astype(BF16).astype(F32)
        middle = (factor - high).astype(BF16).astype(F32)
        low = (factor - high - middle).astype(BF16).astype(F32)
        table_ref[c : c + 1, :] = jnp.concatenate([high, middle], axis=1)
        table_ref[8 + c : 9 + c, :n_sec] = low
        shifts = jnp.where(lane == c, shift.astype(F32), shifts)
    table_ref[15:16, :] = shifts
    payload_ref[ROWS:, :] = table_ref[...].astype(BF16)


def turn(psi_ref, turned_ref, block_ref, sem):
    core = lax.rem(lax.axis_index("sec"), 2)
    copy = pltpu.make_async_copy(psi_ref.at[0, pl.ds(lax.axis_index("term") * G, G)], block_ref, sem)
    copy.start()
    copy.wait()
    for i in range(H):
        turned_ref[i * M : (i + 1) * M, :] = block_ref[2 * i + core].T
        turned_ref[(H + i) * M : (H + i + 1) * M, :] = block_ref[2 * i + 1 - core].T


def fill(psi_ref, near_ref, turned_ref, inner_ref, far_ref):
    psi_ref[0] = near_ref[H * M :, :]
    psi_ref[1] = turned_ref[: H * M, :]
    psi_ref[2] = inner_ref[...]
    psi_ref[3] = far_ref[...]


def left_sums(first_row, slots, psi_ref, out_ref):
    t = lax.axis_index("term")
    core = lax.rem(lax.axis_index("sec"), 2)
    sector = lax.broadcasted_iota(jnp.int32, (M, H * M), 0)
    wanted = lax.broadcasted_iota(jnp.int32, (M, H * M), 1) // M * 2 + t * G + core
    pick = jnp.where((sector == wanted) | (sector == wanted + M // 2), 1.0, 0.0).astype(BF16)
    for w in range(slots.shape[0]):
        table = slots[w, ROWS : ROWS + 16, :]
        spread = jnp.dot(table, pick, preferred_element_type=F32)
        factors = spread[:8] + spread[8:]
        shifts = table.astype(F32)[15:16, :]
        rows = [first_row + shifts[0, c].astype(jnp.int32) * (1 - 2 * core) for c in range(LB)]
        for start in range(0, H * M, 2 * M):
            totals = [None, None]
            for c in range(LB):
                product = lax.dot_general(
                    psi_ref[rows[c], start : start + 2 * M, :],
                    slots[w, c * M : (c + 1) * M, :],
                    (((1,), (1,)), ((), ())),
                    preferred_element_type=F32,
                )
                for h in range(2):
                    at = start + h * M
                    term = product[h * M : (h + 1) * M] * factors[c : c + 1, at : at + M]
                    totals[h] = term if totals[h] is None else totals[h] + term
            for h in range(2):
                out_ref[start // M + h, w * M : (w + 1) * M, :] = totals[h].astype(BF16)


def left_products(own_slots, other_slots, near_ref, turned_ref, inner_ref, far_ref, own_ref, other_ref, psi_ref):
    fill(psi_ref, near_ref, turned_ref, inner_ref, far_ref)
    left_sums(1, own_slots, psi_ref, own_ref)
    left_sums(2, other_slots, psi_ref, other_ref)


def right_products(allowed_ref, right_ref, own_same, other_same, own_next, other_next, out_ref):
    s, t = lax.axis_index("sec"), lax.axis_index("term")
    core = lax.rem(s, 2)
    parity = lax.rem(t, 2)
    for i in range(H):
        same = jnp.concatenate([right_ref[right_chip(t, 2 * m + parity, i)] for m in range(NW // 2)], axis=1)
        following = jnp.concatenate([right_ref[right_chip(t, 2 * m + 1 - parity, i)] for m in range(NW // 2)], axis=1)
        for same_ref, next_ref, which in ((own_same, own_next, core), (other_same, other_next, 1 - core)):
            total = jnp.dot(same, same_ref[i], preferred_element_type=F32)
            total += jnp.dot(following, next_ref[i], preferred_element_type=F32)
            keep = allowed_ref[s - core + which, t * G + 2 * i + core].astype(F32)
            value = (total * keep).T.astype(BF16)
            out_ref[i, which] = value
            out_ref[H + i, which] = value


def on_device(wavefunction, left_env, right_env, coupling, left_shift, allowed, *, n_sec, n_term):
    s, t = lax.axis_index("sec"), lax.axis_index("term")
    groups = n_sec // G

    def device(sec, term):
        return sec * n_term + term

    spread = [
        (device(b, w), device(2 * right_chip(b // G, w, b % G // 2) + b % 2, b // G))
        for b in range(n_sec)
        for w in range(n_term)
    ]
    by_core = [[2 * chip + core for chip in range(n_sec // 2)] for core in range(2)]
    exchange = []
    for core in range(2):

        def members(A, B):
            return [device(A * G + 2 * i + core, B) for i in range(H)]

        exchange += [members(A, B) + members(B, A) for A in range(groups) for B in range(A + 1, groups)]
        exchange += [members(A, A) + members(A + 1, A + 1) for A in range(0, groups, 2)]

    right = lax.ppermute(right_env[0], BOTH, spread)
    payload = pl.pallas_call(
        pack,
        out_shape=jax.ShapeDtypeStruct((ROWS + 16, M), BF16),
        in_specs=[SMEM] + [VMEM] * 3,
        out_specs=VMEM,
        scratch_shapes=[pltpu.VMEM((16, M), F32)],
        compiler_params=PARAMS,
    )(left_shift, left_env.reshape(ROWS, M), coupling[0], allowed)
    turned = pl.pallas_call(
        turn,
        out_shape=jax.ShapeDtypeStruct((G * M, M), BF16),
        in_specs=[pl.BlockSpec(memory_space=pl.ANY)],
        out_specs=VMEM,
        scratch_shapes=[pltpu.VMEM((G, M, M), BF16), pltpu.SemaphoreType.DMA],
        compiler_params=PARAMS,
    )(wavefunction)

    across = [(i, i ^ 1) for i in range(n_sec)]
    near = lax.ppermute(turned, "sec", [(i, i + 1) if i % 2 else (i, i - 1) for i in range(1, n_sec - 1)])
    same = lax.all_gather(
        payload, "term", axis_index_groups=[list(range(parity, n_term, 2)) for parity in range(2)]
    )
    right, near, same = together(right, near, same)
    following = lax.ppermute(same, "term", [(i, i ^ 1) for i in range(n_term)])
    right = lax.all_to_all(
        jnp.tile(right, (n_sec // 2, 1, 1)), "sec", 0, 0, axis_index_groups=by_core, tiled=True
    )
    inner = lax.ppermute(turned[H * M :], "sec", across)
    far = lax.ppermute(near[: H * M], "sec", across)

    def left_call(slots):
        return pl.pallas_call(
            left_products,
            out_shape=[jax.ShapeDtypeStruct((H, NW // 2 * M, M), BF16)] * 2,
            in_specs=[VMEM] * 6,
            out_specs=[VMEM] * 2,
            scratch_shapes=[pltpu.VMEM((4, H * M, M), BF16)],
            compiler_params=PARAMS,
            cost_estimate=pl.CostEstimate(flops=2 * 160 * M**3, bytes_accessed=3 << 20, transcendentals=0),
        )(slots, lax.ppermute(slots, "sec", across), near, turned, inner, far)

    own_same, other_same = left_call(same)
    following, own_same = together(following, own_same)
    own_next, other_next = left_call(following)
    right, own_next = together(right, own_next)
    results = pl.pallas_call(
        right_products,
        out_shape=jax.ShapeDtypeStruct((G, 2, M, M), BF16),
        in_specs=[SMEM] + [VMEM] * 5,
        out_specs=VMEM,
        compiler_params=PARAMS,
        cost_estimate=pl.CostEstimate(flops=2 * 64 * M**3, bytes_accessed=4 << 20, transcendentals=0),
    )(allowed, right, own_same, other_same, own_next, other_next)

    received = lax.all_to_all(results, BOTH, 0, 0, axis_index_groups=exchange, tiled=True)
    A = s // G
    first = jnp.where(A < t, H, jnp.where(A > t, 0, lax.rem(A, 2) * H))
    return lax.dynamic_slice_in_dim(received, first, H, 0).reshape(G, 1, M, M)


def solution(mesh):
    in_specs = (
        P("sec", None, None, None),
        P("term", None, "sec", None, None),
        P("term", "sec", None, None),
        P("term", None, None, None),
        P("term", None),
        P(),
    )
    body = functools.partial(on_device, n_sec=mesh.shape["sec"], n_term=mesh.shape["term"])
    return jax.shard_map(
        body, mesh=mesh, in_specs=in_specs, out_specs=P("term", "sec", None, None), check_vma=False
    )
```

```python
import functools

import jax
import jax.numpy as jnp
from jax import lax
from jax.experimental import pallas as pl
from jax.experimental.pallas import tpu as pltpu
from jax.sharding import PartitionSpec as P

M = 128
LB = 5
NW = 8
G = 8
H = G // 2
BOTH = ("sec", "term")
ROWS = LB * M
F32 = jnp.float32
BF16 = jnp.bfloat16
VMEM = pl.BlockSpec(memory_space=pltpu.VMEM)
SMEM = pl.BlockSpec(memory_space=pltpu.SMEM)
ANY = pl.BlockSpec(memory_space=pl.ANY)
WEIGHTS = (320, 4000)
PARAMS = pltpu.CompilerParams(vmem_limit_bytes=56 * 1024 * 1024)


def together(*arrays):
    return lax.optimization_barrier(arrays)


def right_chip(t, w, i):
    ahead = (w - t) & 7
    far = ahead >> 2
    pair = far * (ahead - 4) + (1 - far) * (3 - ahead)
    x = ((t >> 1) + (pair ^ (pair >> 1))) & 3
    y = (4 * (t & 1) + far * (-1, 1, 2, 4)[i] + (1 - far) * (-2, 0, 3, 5)[i]) & 7
    return x * 8 + y


def pack(shift_ref, env_ref, coupling_ref, allowed_ref, payload_ref, table_ref):
    s = lax.axis_index("sec")
    n_sec = allowed_ref.shape[0]
    payload_ref[:ROWS, :] = env_ref[...]
    table_ref[...] = jnp.zeros_like(table_ref)
    lane = lax.broadcasted_iota(jnp.int32, (1, M), 1)
    shifts = jnp.zeros((1, M), F32)
    for c in range(LB):
        shift = shift_ref[0, c]
        source = s + shift
        inside = jnp.logical_and(source >= 0, source < n_sec).astype(F32)
        kept = allowed_ref[pl.ds(jnp.clip(source, 0, n_sec - 1), 1), :].astype(F32) * inside
        factor = coupling_ref[c, pl.ds(s, 1), :] * kept
        high = factor.astype(BF16).astype(F32)
        middle = (factor - high).astype(BF16).astype(F32)
        low = (factor - high - middle).astype(BF16).astype(F32)
        table_ref[c : c + 1, :] = jnp.concatenate([high, middle], axis=1)
        table_ref[8 + c : 9 + c, :n_sec] = low
        shifts = jnp.where(lane == c, shift.astype(F32), shifts)
    table_ref[15:16, :] = shifts
    payload_ref[ROWS:, :] = table_ref[...].astype(BF16)


def turn(psi_ref, turned_ref, block_ref, sem):
    core = lax.rem(lax.axis_index("sec"), 2)
    copy = pltpu.make_async_copy(psi_ref.at[0, pl.ds(lax.axis_index("term") * G, G)], block_ref, sem)
    copy.start()
    copy.wait()
    for i in range(H):
        turned_ref[i * M : (i + 1) * M, :] = block_ref[2 * i + core].T
        turned_ref[(H + i) * M : (H + i + 1) * M, :] = block_ref[2 * i + 1 - core].T


def fill(psi_ref, near_ref, turned_ref, inner_ref, far_ref):
    psi_ref[0] = near_ref[H * M :, :]
    psi_ref[1] = turned_ref[: H * M, :]
    psi_ref[2] = inner_ref[...]
    psi_ref[3] = far_ref[...]


def left_sums(first_row, slots, psi_ref, out_ref):
    t = lax.axis_index("term")
    core = lax.rem(lax.axis_index("sec"), 2)
    sector = lax.broadcasted_iota(jnp.int32, (M, H * M), 0)
    wanted = lax.broadcasted_iota(jnp.int32, (M, H * M), 1) // M * 2 + t * G + core
    pick = jnp.where((sector == wanted) | (sector == wanted + M // 2), 1.0, 0.0).astype(BF16)
    for w in range(slots.shape[0]):
        table = slots[w, ROWS : ROWS + 16, :]
        spread = jnp.dot(table, pick, preferred_element_type=F32)
        factors = spread[:8] + spread[8:]
        shifts = table.astype(F32)[15:16, :]
        rows = [first_row + shifts[0, c].astype(jnp.int32) * (1 - 2 * core) for c in range(LB)]
        for start in range(0, H * M, 2 * M):
            totals = [None, None]
            for c in range(LB):
                product = lax.dot_general(
                    psi_ref[rows[c], start : start + 2 * M, :],
                    slots[w, c * M : (c + 1) * M, :],
                    (((1,), (1,)), ((), ())),
                    preferred_element_type=F32,
                )
                for h in range(2):
                    at = start + h * M
                    term = product[h * M : (h + 1) * M] * factors[c : c + 1, at : at + M]
                    totals[h] = term if totals[h] is None else totals[h] + term
            for h in range(2):
                out_ref[start // M + h, w * M : (w + 1) * M, :] = totals[h].astype(BF16)


def left_products(
    own_slots, other_hbm, near_ref, turned_ref, inner_ref, far_ref, own_ref, other_ref, psi_ref, other_slots, sem
):
    copy = pltpu.make_async_copy(other_hbm, other_slots, sem)
    copy.start()
    fill(psi_ref, near_ref, turned_ref, inner_ref, far_ref)
    left_sums(1, own_slots, psi_ref, own_ref)
    copy.wait()
    left_sums(2, other_slots, psi_ref, other_ref)


def right_products(allowed_ref, *refs):
    arrays, out_ref, held, sems = refs[:5], refs[5], refs[6:11], refs[11]
    copies = [pltpu.make_async_copy(arrays[n], held[n], sems.at[n]) for n in range(5)]
    for copy in copies:
        copy.start()
    for copy in copies:
        copy.wait()
    right_ref, own_same, other_same, own_next, other_next = held
    s, t = lax.axis_index("sec"), lax.axis_index("term")
    core = lax.rem(s, 2)
    parity = lax.rem(t, 2)
    for i in range(H):
        same = jnp.concatenate([right_ref[right_chip(t, 2 * m + parity, i)] for m in range(NW // 2)], axis=1)
        following = jnp.concatenate([right_ref[right_chip(t, 2 * m + 1 - parity, i)] for m in range(NW // 2)], axis=1)
        for same_ref, next_ref, which in ((own_same, own_next, core), (other_same, other_next, 1 - core)):
            total = jnp.dot(same, same_ref[i], preferred_element_type=F32)
            total += jnp.dot(following, next_ref[i], preferred_element_type=F32)
            keep = allowed_ref[s - core + which, t * G + 2 * i + core].astype(F32)
            value = (total * keep).T.astype(BF16)
            out_ref[i, which] = value
            out_ref[H + i, which] = value


def on_device(wavefunction, left_env, right_env, coupling, left_shift, allowed, *, n_sec, n_term):
    s, t = lax.axis_index("sec"), lax.axis_index("term")
    groups = n_sec // G

    def device(sec, term):
        return sec * n_term + term

    spread = [
        (device(b, w), device(2 * right_chip(b // G, w, b % G // 2) + b % 2, b // G))
        for b in range(n_sec)
        for w in range(n_term)
    ]
    by_core = [[2 * chip + core for chip in range(n_sec // 2)] for core in range(2)]
    exchange = []
    for core in range(2):

        def members(A, B):
            return [device(A * G + 2 * i + core, B) for i in range(H)]

        exchange += [members(A, B) + members(B, A) for A in range(groups) for B in range(A + 1, groups)]
        exchange += [members(A, A) + members(A + 1, A + 1) for A in range(0, groups, 2)]

    right = lax.ppermute(right_env[0], BOTH, spread)
    payload = pl.pallas_call(
        pack,
        out_shape=jax.ShapeDtypeStruct((ROWS + 16, M), BF16),
        in_specs=[SMEM] + [VMEM] * 3,
        out_specs=VMEM,
        scratch_shapes=[pltpu.VMEM((16, M), F32)],
        compiler_params=PARAMS,
    )(left_shift, left_env.reshape(ROWS, M), coupling[0], allowed)
    turned = pl.pallas_call(
        turn,
        out_shape=jax.ShapeDtypeStruct((G * M, M), BF16),
        in_specs=[ANY],
        out_specs=VMEM,
        scratch_shapes=[pltpu.VMEM((G, M, M), BF16), pltpu.SemaphoreType.DMA],
        compiler_params=PARAMS,
    )(wavefunction)

    across = [(i, i ^ 1) for i in range(n_sec)]
    near = lax.ppermute(turned, "sec", [(i, i + 1) if i % 2 else (i, i - 1) for i in range(1, n_sec - 1)])
    same = lax.all_gather(
        payload, "term", axis_index_groups=[list(range(parity, n_term, 2)) for parity in range(2)]
    )
    right, near, same = together(right, near, same)
    following = lax.ppermute(same, "term", [(i, i ^ 1) for i in range(n_term)])
    right = lax.all_to_all(
        jnp.tile(right, (n_sec // 2, 1, 1)), "sec", 0, 0, axis_index_groups=by_core, tiled=True
    )
    inner = lax.ppermute(turned[H * M :], "sec", across)
    far = lax.ppermute(near[: H * M], "sec", across)

    def left_call(slots, weight):
        return pl.pallas_call(
            left_products,
            out_shape=[jax.ShapeDtypeStruct((H, NW // 2 * M, M), BF16)] * 2,
            in_specs=[VMEM, ANY] + [VMEM] * 4,
            out_specs=[VMEM] * 2,
            scratch_shapes=[
                pltpu.VMEM((4, H * M, M), BF16),
                pltpu.VMEM((NW // 2, ROWS + 16, M), BF16),
                pltpu.SemaphoreType.DMA,
            ],
            compiler_params=PARAMS,
            cost_estimate=pl.CostEstimate(flops=weight * M**3, bytes_accessed=3 << 20, transcendentals=0),
        )(slots, lax.ppermute(slots, "sec", across), near, turned, inner, far)

    own_same, other_same = left_call(same, WEIGHTS[0])
    following, own_same = together(following, own_same)
    own_next, other_next = left_call(following, WEIGHTS[1])
    right, own_next = together(right, own_next)
    results = pl.pallas_call(
        right_products,
        out_shape=jax.ShapeDtypeStruct((G, 2, M, M), BF16),
        in_specs=[SMEM] + [ANY] * 5,
        out_specs=VMEM,
        scratch_shapes=[pltpu.VMEM((n_sec // 2, M, M), BF16)]
        + [pltpu.VMEM((H, NW // 2 * M, M), BF16)] * 4
        + [pltpu.SemaphoreType.DMA((5,))],
        compiler_params=PARAMS,
        cost_estimate=pl.CostEstimate(flops=2 * 64 * M**3, bytes_accessed=4 << 20, transcendentals=0),
    )(allowed, right, own_same, other_same, own_next, other_next)

    received = lax.all_to_all(results, BOTH, 0, 0, axis_index_groups=exchange, tiled=True)
    A = s // G
    first = jnp.where(A < t, H, jnp.where(A > t, 0, lax.rem(A, 2) * H))
    return lax.dynamic_slice_in_dim(received, first, H, 0).reshape(G, 1, M, M)


def solution(mesh):
    in_specs = (
        P("sec", None, None, None),
        P("term", None, "sec", None, None),
        P("term", "sec", None, None),
        P("term", None, None, None),
        P("term", None),
        P(),
    )
    body = functools.partial(on_device, n_sec=mesh.shape["sec"], n_term=mesh.shape["term"])
    return jax.shard_map(
        body, mesh=mesh, in_specs=in_specs, out_specs=P("term", "sec", None, None), check_vma=False
    )
```

```python
import functools

import jax
import jax.numpy as jnp
from jax import lax
from jax.experimental import pallas as pl
from jax.experimental.pallas import tpu as pltpu
from jax.sharding import PartitionSpec as P

M = 128
LB = 5
NW = 8
G = 8
H = G // 2
BOTH = ("sec", "term")
ROWS = LB * M
F32 = jnp.float32
BF16 = jnp.bfloat16
VMEM = pl.BlockSpec(memory_space=pltpu.VMEM)
SMEM = pl.BlockSpec(memory_space=pltpu.SMEM)
PARAMS = pltpu.CompilerParams(vmem_limit_bytes=56 * 1024 * 1024)


def together(*arrays):
    return lax.optimization_barrier(arrays)


def right_chip(t, w, i):
    ahead = (w - t) & 7
    far = ahead >> 2
    pair = far * (ahead - 4) + (1 - far) * (3 - ahead)
    x = ((t >> 1) + (pair ^ (pair >> 1))) & 3
    y = (4 * (t & 1) + far * (-1, 1, 2, 4)[i] + (1 - far) * (-2, 0, 3, 5)[i]) & 7
    return x * 8 + y


def pack(shift_ref, env_ref, coupling_ref, allowed_ref, payload_ref, table_ref):
    s = lax.axis_index("sec")
    n_sec = allowed_ref.shape[0]
    payload_ref[:ROWS, :] = env_ref[...]
    table_ref[...] = jnp.zeros_like(table_ref)
    lane = lax.broadcasted_iota(jnp.int32, (1, M), 1)
    shifts = jnp.zeros((1, M), F32)
    for c in range(LB):
        shift = shift_ref[0, c]
        source = s + shift
        inside = jnp.logical_and(source >= 0, source < n_sec).astype(F32)
        kept = allowed_ref[pl.ds(jnp.clip(source, 0, n_sec - 1), 1), :].astype(F32) * inside
        factor = coupling_ref[c, pl.ds(s, 1), :] * kept
        high = factor.astype(BF16).astype(F32)
        middle = (factor - high).astype(BF16).astype(F32)
        low = (factor - high - middle).astype(BF16).astype(F32)
        table_ref[c : c + 1, :] = jnp.concatenate([high, middle], axis=1)
        table_ref[8 + c : 9 + c, :n_sec] = low
        shifts = jnp.where(lane == c, shift.astype(F32), shifts)
    table_ref[15:16, :] = shifts
    payload_ref[ROWS:, :] = table_ref[...].astype(BF16)


def turn(psi_ref, turned_ref, block_ref, sem):
    core = lax.rem(lax.axis_index("sec"), 2)
    copy = pltpu.make_async_copy(psi_ref.at[0, pl.ds(lax.axis_index("term") * G, G)], block_ref, sem)
    copy.start()
    copy.wait()
    for i in range(H):
        turned_ref[i * M : (i + 1) * M, :] = block_ref[2 * i + core].T
        turned_ref[(H + i) * M : (H + i + 1) * M, :] = block_ref[2 * i + 1 - core].T


def fill(psi_ref, near_ref, turned_ref, inner_ref, far_ref):
    psi_ref[0] = near_ref[H * M :, :]
    psi_ref[1] = turned_ref[: H * M, :]
    psi_ref[2] = inner_ref[...]
    psi_ref[3] = far_ref[...]


def left_sums(first_row, slots, psi_ref, out_ref):
    t = lax.axis_index("term")
    core = lax.rem(lax.axis_index("sec"), 2)
    sector = lax.broadcasted_iota(jnp.int32, (M, H * M), 0)
    wanted = lax.broadcasted_iota(jnp.int32, (M, H * M), 1) // M * 2 + t * G + core
    pick = jnp.where((sector == wanted) | (sector == wanted + M // 2), 1.0, 0.0).astype(BF16)
    for w in range(NW):
        table = slots[w, ROWS : ROWS + 16, :]
        spread = jnp.dot(table, pick, preferred_element_type=F32)
        factors = spread[:8] + spread[8:]
        shifts = table.astype(F32)[15:16, :]
        rows = [first_row + shifts[0, c].astype(jnp.int32) * (1 - 2 * core) for c in range(LB)]
        for start in range(0, H * M, 2 * M):
            totals = [None, None]
            for c in range(LB):
                product = lax.dot_general(
                    psi_ref[rows[c], start : start + 2 * M, :],
                    slots[w, c * M : (c + 1) * M, :],
                    (((1,), (1,)), ((), ())),
                    preferred_element_type=F32,
                )
                for h in range(2):
                    at = start + h * M
                    term = product[h * M : (h + 1) * M] * factors[c : c + 1, at : at + M]
                    totals[h] = term if totals[h] is None else totals[h] + term
            for h in range(2):
                out_ref[start // M + h, w * M : (w + 1) * M, :] = totals[h].astype(BF16)


def own_products(slots, near_ref, turned_ref, inner_ref, far_ref, out_ref, psi_ref):
    fill(psi_ref, near_ref, turned_ref, inner_ref, far_ref)
    left_sums(1, slots, psi_ref, out_ref)


def all_products(allowed_ref, slots, near_ref, turned_ref, inner_ref, far_ref, right_ref, own_ref, out_ref, psi_ref, other_ref):
    fill(psi_ref, near_ref, turned_ref, inner_ref, far_ref)
    left_sums(2, slots, psi_ref, other_ref)
    s, t = lax.axis_index("sec"), lax.axis_index("term")
    core = lax.rem(s, 2)
    for i in range(H):
        right = jnp.concatenate([right_ref[right_chip(t, w, i)] for w in range(NW)], axis=1)
        for partial_ref, which in ((own_ref, core), (other_ref, 1 - core)):
            total = jnp.dot(right, partial_ref[i], preferred_element_type=F32)
            keep = allowed_ref[s - core + which, t * G + 2 * i + core].astype(F32)
            value = (total * keep).T.astype(BF16)
            out_ref[i, which] = value
            out_ref[H + i, which] = value


def on_device(wavefunction, left_env, right_env, coupling, left_shift, allowed, *, n_sec, n_term):
    s, t = lax.axis_index("sec"), lax.axis_index("term")
    groups = n_sec // G

    def device(sec, term):
        return sec * n_term + term

    spread = [
        (device(b, w), device(2 * right_chip(b // G, w, b % G // 2) + b % 2, b // G))
        for b in range(n_sec)
        for w in range(n_term)
    ]
    by_core = [[2 * chip + core for chip in range(n_sec // 2)] for core in range(2)]
    exchange = []
    for core in range(2):

        def members(A, B):
            return [device(A * G + 2 * i + core, B) for i in range(H)]

        exchange += [members(A, B) + members(B, A) for A in range(groups) for B in range(A + 1, groups)]
        exchange += [members(A, A) + members(A + 1, A + 1) for A in range(0, groups, 2)]

    right = lax.ppermute(right_env[0], BOTH, spread)
    payload = pl.pallas_call(
        pack,
        out_shape=jax.ShapeDtypeStruct((ROWS + 16, M), BF16),
        in_specs=[SMEM] + [VMEM] * 3,
        out_specs=VMEM,
        scratch_shapes=[pltpu.VMEM((16, M), F32)],
        compiler_params=PARAMS,
    )(left_shift, left_env.reshape(ROWS, M), coupling[0], allowed)
    turned = pl.pallas_call(
        turn,
        out_shape=jax.ShapeDtypeStruct((G * M, M), BF16),
        in_specs=[pl.BlockSpec(memory_space=pl.ANY)],
        out_specs=VMEM,
        scratch_shapes=[pltpu.VMEM((G, M, M), BF16), pltpu.SemaphoreType.DMA],
        compiler_params=PARAMS,
    )(wavefunction)

    payloads = lax.all_gather(payload, "term")
    across = [(i, i ^ 1) for i in range(n_sec)]
    near = lax.ppermute(turned, "sec", [(i, i + 1) if i % 2 else (i, i - 1) for i in range(1, n_sec - 1)])
    right, near = together(right, near)
    inner = lax.ppermute(turned[H * M :], "sec", across)
    far = lax.ppermute(near[: H * M], "sec", across)
    right = lax.all_to_all(
        jnp.tile(right, (n_sec // 2, 1, 1)), "sec", 0, 0, axis_index_groups=by_core, tiled=True
    )
    payloads, inner, far = together(payloads, inner, far)
    other_payloads = lax.ppermute(payloads, "sec", across)

    own = pl.pallas_call(
        own_products,
        out_shape=jax.ShapeDtypeStruct((H, NW * M, M), BF16),
        in_specs=[VMEM] * 5,
        out_specs=VMEM,
        scratch_shapes=[pltpu.VMEM((4, H * M, M), BF16)],
        compiler_params=PARAMS,
        cost_estimate=pl.CostEstimate(flops=2 * 160 * M**3, bytes_accessed=3 << 20, transcendentals=0),
    )(payloads, near, turned, inner, far)
    results = pl.pallas_call(
        all_products,
        out_shape=jax.ShapeDtypeStruct((G, 2, M, M), BF16),
        in_specs=[SMEM] + [VMEM] * 7,
        out_specs=VMEM,
        scratch_shapes=[pltpu.VMEM((4, H * M, M), BF16), pltpu.VMEM((H, NW * M, M), BF16)],
        compiler_params=PARAMS,
        cost_estimate=pl.CostEstimate(flops=2 * 224 * M**3, bytes_accessed=6 << 20, transcendentals=0),
    )(allowed, other_payloads, near, turned, inner, far, right, own)

    received = lax.all_to_all(results, BOTH, 0, 0, axis_index_groups=exchange, tiled=True)
    A = s // G
    first = jnp.where(A < t, H, jnp.where(A > t, 0, lax.rem(A, 2) * H))
    return lax.dynamic_slice_in_dim(received, first, H, 0).reshape(G, 1, M, M)


def solution(mesh):
    in_specs = (
        P("sec", None, None, None),
        P("term", None, "sec", None, None),
        P("term", "sec", None, None),
        P("term", None, None, None),
        P("term", None),
        P(),
    )
    body = functools.partial(on_device, n_sec=mesh.shape["sec"], n_term=mesh.shape["term"])
    return jax.shard_map(
        body, mesh=mesh, in_specs=in_specs, out_specs=P("term", "sec", None, None), check_vma=False
    )
```

```python
import functools

import jax
import jax.numpy as jnp
from jax import lax
from jax.experimental import pallas as pl
from jax.experimental.pallas import tpu as pltpu
from jax.sharding import PartitionSpec as P

M = 128
LB = 5
NW = 8
G = 8
H = G // 2
BOTH = ("sec", "term")
ROWS = LB * M
F32 = jnp.float32
BF16 = jnp.bfloat16
VMEM = pl.BlockSpec(memory_space=pltpu.VMEM)
SMEM = pl.BlockSpec(memory_space=pltpu.SMEM)
PARAMS = pltpu.CompilerParams(vmem_limit_bytes=16 * 1024 * 1024)


def together(*arrays):
    return lax.optimization_barrier(arrays)


def right_chip(t, w, i):
    ahead = (w - t) & 7
    far = ahead >> 2
    pair = far * (ahead - 4) + (1 - far) * (3 - ahead)
    x = ((t >> 1) + (pair ^ (pair >> 1))) & 3
    y = (4 * (t & 1) + far * (-1, 1, 2, 4)[i] + (1 - far) * (-2, 0, 3, 5)[i]) & 7
    return x * 8 + y


def pack(shift_ref, env_ref, coupling_ref, allowed_ref, payload_ref, table_ref):
    s = lax.axis_index("sec")
    n_sec = allowed_ref.shape[0]
    payload_ref[:ROWS, :] = env_ref[...]
    table_ref[...] = jnp.zeros_like(table_ref)
    lane = lax.broadcasted_iota(jnp.int32, (1, M), 1)
    shifts = jnp.zeros((1, M), F32)
    for c in range(LB):
        shift = shift_ref[0, c]
        source = s + shift
        inside = jnp.logical_and(source >= 0, source < n_sec).astype(F32)
        kept = allowed_ref[pl.ds(jnp.clip(source, 0, n_sec - 1), 1), :].astype(F32) * inside
        factor = coupling_ref[c, pl.ds(s, 1), :] * kept
        high = factor.astype(BF16).astype(F32)
        middle = (factor - high).astype(BF16).astype(F32)
        low = (factor - high - middle).astype(BF16).astype(F32)
        table_ref[c : c + 1, :] = jnp.concatenate([high, middle], axis=1)
        table_ref[8 + c : 9 + c, :n_sec] = low
        shifts = jnp.where(lane == c, shift.astype(F32), shifts)
    table_ref[15:16, :] = shifts
    payload_ref[ROWS:, :] = table_ref[...].astype(BF16)


def turn(psi_ref, turned_ref, block_ref, sem):
    core = lax.rem(lax.axis_index("sec"), 2)
    copy = pltpu.make_async_copy(psi_ref.at[0, pl.ds(lax.axis_index("term") * G, G)], block_ref, sem)
    copy.start()
    copy.wait()
    for i in range(H):
        turned_ref[i * M : (i + 1) * M, :] = block_ref[2 * i + core].T
        turned_ref[(H + i) * M : (H + i + 1) * M, :] = block_ref[2 * i + 1 - core].T


def fill(psi_ref, near_ref, turned_ref, inner_ref, far_ref):
    psi_ref[0] = near_ref[H * M :, :]
    psi_ref[1] = turned_ref[: H * M, :]
    psi_ref[2] = inner_ref[...]
    psi_ref[3] = far_ref[...]


def left_sums(first_row, slots, psi_ref, out_ref):
    t = lax.axis_index("term")
    core = lax.rem(lax.axis_index("sec"), 2)
    sector = lax.broadcasted_iota(jnp.int32, (M, H * M), 0)
    wanted = lax.broadcasted_iota(jnp.int32, (M, H * M), 1) // M * 2 + t * G + core
    pick = jnp.where((sector == wanted) | (sector == wanted + M // 2), 1.0, 0.0).astype(BF16)
    for w in range(NW):
        table = slots[w, ROWS : ROWS + 16, :]
        spread = jnp.dot(table, pick, preferred_element_type=F32)
        factors = spread[:8] + spread[8:]
        shifts = table.astype(F32)[15:16, :]
        rows = [first_row + shifts[0, c].astype(jnp.int32) * (1 - 2 * core) for c in range(LB)]
        for start in range(0, H * M, 2 * M):
            totals = [None, None]
            for c in range(LB):
                product = lax.dot_general(
                    psi_ref[rows[c], start : start + 2 * M, :],
                    slots[w, c * M : (c + 1) * M, :],
                    (((1,), (1,)), ((), ())),
                    preferred_element_type=F32,
                )
                for h in range(2):
                    at = start + h * M
                    term = product[h * M : (h + 1) * M] * factors[c : c + 1, at : at + M]
                    totals[h] = term if totals[h] is None else totals[h] + term
            for h in range(2):
                out_ref[start // M + h, w * M : (w + 1) * M, :] = totals[h].astype(BF16)


def own_products(slots, near_ref, turned_ref, inner_ref, far_ref, out_ref, psi_ref):
    fill(psi_ref, near_ref, turned_ref, inner_ref, far_ref)
    left_sums(1, slots, psi_ref, out_ref)


def all_products(allowed_ref, slots, near_ref, turned_ref, inner_ref, far_ref, right_ref, own_ref, out_ref, psi_ref, other_ref):
    fill(psi_ref, near_ref, turned_ref, inner_ref, far_ref)
    left_sums(2, slots, psi_ref, other_ref)
    s, t = lax.axis_index("sec"), lax.axis_index("term")
    core = lax.rem(s, 2)
    for i in range(H):
        right = jnp.concatenate([right_ref[right_chip(t, w, i)] for w in range(NW)], axis=1)
        for partial_ref, which in ((own_ref, core), (other_ref, 1 - core)):
            total = jnp.dot(right, partial_ref[i], preferred_element_type=F32)
            keep = allowed_ref[s - core + which, t * G + 2 * i + core].astype(F32)
            value = (total * keep).T.astype(BF16)
            out_ref[i, which] = value
            out_ref[H + i, which] = value


def on_device(wavefunction, left_env, right_env, coupling, left_shift, allowed, *, n_sec, n_term):
    s, t = lax.axis_index("sec"), lax.axis_index("term")
    groups = n_sec // G

    def device(sec, term):
        return sec * n_term + term

    spread = [
        (device(b, w), device(2 * right_chip(b // G, w, b % G // 2) + b % 2, b // G))
        for b in range(n_sec)
        for w in range(n_term)
    ]
    by_core = [[2 * chip + core for chip in range(n_sec // 2)] for core in range(2)]
    exchange = []
    for core in range(2):

        def members(A, B):
            return [device(A * G + 2 * i + core, B) for i in range(H)]

        exchange += [members(A, B) + members(B, A) for A in range(groups) for B in range(A + 1, groups)]
        exchange += [members(A, A) + members(A + 1, A + 1) for A in range(0, groups, 2)]

    right = lax.ppermute(right_env[0], BOTH, spread)
    payload = pl.pallas_call(
        pack,
        out_shape=jax.ShapeDtypeStruct((ROWS + 16, M), BF16),
        in_specs=[SMEM] + [VMEM] * 3,
        out_specs=VMEM,
        scratch_shapes=[pltpu.VMEM((16, M), F32)],
        compiler_params=PARAMS,
    )(left_shift, left_env.reshape(ROWS, M), coupling[0], allowed)
    turned = pl.pallas_call(
        turn,
        out_shape=jax.ShapeDtypeStruct((G * M, M), BF16),
        in_specs=[pl.BlockSpec(memory_space=pl.ANY)],
        out_specs=VMEM,
        scratch_shapes=[pltpu.VMEM((G, M, M), BF16), pltpu.SemaphoreType.DMA],
        compiler_params=PARAMS,
    )(wavefunction)

    payloads = lax.all_gather(payload, "term")
    across = [(i, i ^ 1) for i in range(n_sec)]
    near = lax.ppermute(turned, "sec", [(i, i + 1) if i % 2 else (i, i - 1) for i in range(1, n_sec - 1)])
    right, near = together(right, near)
    inner = lax.ppermute(turned[H * M :], "sec", across)
    far = lax.ppermute(near[: H * M], "sec", across)
    right = lax.all_to_all(
        jnp.tile(right, (n_sec // 2, 1, 1)), "sec", 0, 0, axis_index_groups=by_core, tiled=True
    )
    payloads, inner, far = together(payloads, inner, far)
    other_payloads = lax.ppermute(payloads, "sec", across)

    own = pl.pallas_call(
        own_products,
        out_shape=jax.ShapeDtypeStruct((H, NW * M, M), BF16),
        in_specs=[VMEM] * 5,
        out_specs=VMEM,
        scratch_shapes=[pltpu.VMEM((4, H * M, M), BF16)],
        compiler_params=PARAMS,
        cost_estimate=pl.CostEstimate(flops=2 * 160 * M**3, bytes_accessed=3 << 20, transcendentals=0),
    )(payloads, near, turned, inner, far)
    results = pl.pallas_call(
        all_products,
        out_shape=jax.ShapeDtypeStruct((G, 2, M, M), BF16),
        in_specs=[SMEM] + [VMEM] * 7,
        out_specs=VMEM,
        scratch_shapes=[pltpu.VMEM((4, H * M, M), BF16), pltpu.VMEM((H, NW * M, M), BF16)],
        compiler_params=PARAMS,
        cost_estimate=pl.CostEstimate(flops=2 * 224 * M**3, bytes_accessed=6 << 20, transcendentals=0),
    )(allowed, other_payloads, near, turned, inner, far, right, own)

    received = lax.all_to_all(results, BOTH, 0, 0, axis_index_groups=exchange, tiled=True)
    A = s // G
    first = jnp.where(A < t, H, jnp.where(A > t, 0, lax.rem(A, 2) * H))
    return lax.dynamic_slice_in_dim(received, first, H, 0).reshape(G, 1, M, M)


def solution(mesh):
    in_specs = (
        P("sec", None, None, None),
        P("term", None, "sec", None, None),
        P("term", "sec", None, None),
        P("term", None, None, None),
        P("term", None),
        P(),
    )
    body = functools.partial(on_device, n_sec=mesh.shape["sec"], n_term=mesh.shape["term"])
    return jax.shard_map(
        body, mesh=mesh, in_specs=in_specs, out_specs=P("term", "sec", None, None), check_vma=False
    )
```

```python
import functools

import jax
import jax.numpy as jnp
from jax import lax
from jax.experimental import pallas as pl
from jax.experimental.pallas import tpu as pltpu
from jax.sharding import PartitionSpec as P

M = 128
LB = 5
NW = 8
G = 8
H = G // 2
BOTH = ("sec", "term")
ROWS = LB * M
F32 = jnp.float32
BF16 = jnp.bfloat16
VMEM = pl.BlockSpec(memory_space=pltpu.VMEM)
SMEM = pl.BlockSpec(memory_space=pltpu.SMEM)
PARAMS = pltpu.CompilerParams(vmem_limit_bytes=16 * 1024 * 1024)
FIRST = pltpu.CompilerParams(vmem_limit_bytes=56 * 1024 * 1024)
SPREAD_COST = 3000


def together(*arrays):
    return lax.optimization_barrier(arrays)


def right_chip(t, w, i):
    ahead = (w - t) & 7
    far = ahead >> 2
    pair = far * (ahead - 4) + (1 - far) * (3 - ahead)
    x = ((t >> 1) + (pair ^ (pair >> 1))) & 3
    y = (4 * (t & 1) + far * (-1, 1, 2, 4)[i] + (1 - far) * (-2, 0, 3, 5)[i]) & 7
    return x * 8 + y


def pack(shift_ref, env_ref, coupling_ref, allowed_ref, payload_ref, table_ref):
    s = lax.axis_index("sec")
    n_sec = allowed_ref.shape[0]
    payload_ref[:ROWS, :] = env_ref[...]
    table_ref[...] = jnp.zeros_like(table_ref)
    lane = lax.broadcasted_iota(jnp.int32, (1, M), 1)
    shifts = jnp.zeros((1, M), F32)
    for c in range(LB):
        shift = shift_ref[0, c]
        source = s + shift
        inside = jnp.logical_and(source >= 0, source < n_sec).astype(F32)
        kept = allowed_ref[pl.ds(jnp.clip(source, 0, n_sec - 1), 1), :].astype(F32) * inside
        factor = coupling_ref[c, pl.ds(s, 1), :] * kept
        high = factor.astype(BF16).astype(F32)
        middle = (factor - high).astype(BF16).astype(F32)
        low = (factor - high - middle).astype(BF16).astype(F32)
        table_ref[c : c + 1, :] = jnp.concatenate([high, middle], axis=1)
        table_ref[8 + c : 9 + c, :n_sec] = low
        shifts = jnp.where(lane == c, shift.astype(F32), shifts)
    table_ref[15:16, :] = shifts
    payload_ref[ROWS:, :] = table_ref[...].astype(BF16)


def turn(psi_ref, turned_ref, block_ref, sem):
    core = lax.rem(lax.axis_index("sec"), 2)
    copy = pltpu.make_async_copy(psi_ref.at[0, pl.ds(lax.axis_index("term") * G, G)], block_ref, sem)
    copy.start()
    copy.wait()
    for i in range(H):
        turned_ref[i * M : (i + 1) * M, :] = block_ref[2 * i + core].T
        turned_ref[(H + i) * M : (H + i + 1) * M, :] = block_ref[2 * i + 1 - core].T


def copies(block_ref, out_ref):
    for n in range(out_ref.shape[0]):
        out_ref[n] = block_ref[0]


def fill(psi_ref, near_ref, turned_ref, inner_ref, far_ref):
    psi_ref[0] = near_ref[H * M :, :]
    psi_ref[1] = turned_ref[: H * M, :]
    psi_ref[2] = inner_ref[...]
    psi_ref[3] = far_ref[...]


def left_sums(first_row, slots, psi_ref, out_ref):
    t = lax.axis_index("term")
    core = lax.rem(lax.axis_index("sec"), 2)
    sector = lax.broadcasted_iota(jnp.int32, (M, H * M), 0)
    wanted = lax.broadcasted_iota(jnp.int32, (M, H * M), 1) // M * 2 + t * G + core
    pick = jnp.where((sector == wanted) | (sector == wanted + M // 2), 1.0, 0.0).astype(BF16)
    for w in range(NW):
        table = slots[w, ROWS : ROWS + 16, :]
        spread = jnp.dot(table, pick, preferred_element_type=F32)
        factors = spread[:8] + spread[8:]
        shifts = table.astype(F32)[15:16, :]
        rows = [first_row + shifts[0, c].astype(jnp.int32) * (1 - 2 * core) for c in range(LB)]
        for start in range(0, H * M, 2 * M):
            totals = [None, None]
            for c in range(LB):
                product = lax.dot_general(
                    psi_ref[rows[c], start : start + 2 * M, :],
                    slots[w, c * M : (c + 1) * M, :],
                    (((1,), (1,)), ((), ())),
                    preferred_element_type=F32,
                )
                for h in range(2):
                    at = start + h * M
                    term = product[h * M : (h + 1) * M] * factors[c : c + 1, at : at + M]
                    totals[h] = term if totals[h] is None else totals[h] + term
            for h in range(2):
                out_ref[start // M + h, w * M : (w + 1) * M, :] = totals[h].astype(BF16)


def own_products(slots, near_ref, turned_ref, inner_ref, far_ref, out_ref, psi_ref):
    fill(psi_ref, near_ref, turned_ref, inner_ref, far_ref)
    left_sums(1, slots, psi_ref, out_ref)


def all_products(allowed_ref, slots, near_ref, turned_ref, inner_ref, far_ref, right_ref, own_ref, out_ref, psi_ref, other_ref):
    fill(psi_ref, near_ref, turned_ref, inner_ref, far_ref)
    left_sums(2, slots, psi_ref, other_ref)
    s, t = lax.axis_index("sec"), lax.axis_index("term")
    core = lax.rem(s, 2)
    for i in range(H):
        right = jnp.concatenate([right_ref[right_chip(t, w, i)] for w in range(NW)], axis=1)
        for partial_ref, which in ((own_ref, core), (other_ref, 1 - core)):
            total = jnp.dot(right, partial_ref[i], preferred_element_type=F32)
            keep = allowed_ref[s - core + which, t * G + 2 * i + core].astype(F32)
            value = (total * keep).T.astype(BF16)
            out_ref[i, which] = value
            out_ref[H + i, which] = value


def on_device(wavefunction, left_env, right_env, coupling, left_shift, allowed, *, n_sec, n_term):
    s, t = lax.axis_index("sec"), lax.axis_index("term")
    groups = n_sec // G

    def device(sec, term):
        return sec * n_term + term

    spread = [
        (device(b, w), device(2 * right_chip(b // G, w, b % G // 2) + b % 2, b // G))
        for b in range(n_sec)
        for w in range(n_term)
    ]
    by_core = [[2 * chip + core for chip in range(n_sec // 2)] for core in range(2)]
    exchange = []
    for core in range(2):

        def members(A, B):
            return [device(A * G + 2 * i + core, B) for i in range(H)]

        exchange += [members(A, B) + members(B, A) for A in range(groups) for B in range(A + 1, groups)]
        exchange += [members(A, A) + members(A + 1, A + 1) for A in range(0, groups, 2)]

    right = lax.ppermute(right_env[0], BOTH, spread)
    payload = pl.pallas_call(
        pack,
        out_shape=jax.ShapeDtypeStruct((ROWS + 16, M), BF16),
        in_specs=[SMEM] + [VMEM] * 3,
        out_specs=VMEM,
        scratch_shapes=[pltpu.VMEM((16, M), F32)],
        compiler_params=FIRST,
    )(left_shift, left_env.reshape(ROWS, M), coupling[0], allowed)
    turned = pl.pallas_call(
        turn,
        out_shape=jax.ShapeDtypeStruct((G * M, M), BF16),
        in_specs=[pl.BlockSpec(memory_space=pl.ANY)],
        out_specs=VMEM,
        scratch_shapes=[pltpu.VMEM((G, M, M), BF16), pltpu.SemaphoreType.DMA],
        compiler_params=FIRST,
    )(wavefunction)

    payloads = lax.all_gather(payload, "term")
    across = [(i, i ^ 1) for i in range(n_sec)]
    near = lax.ppermute(turned, "sec", [(i, i + 1) if i % 2 else (i, i - 1) for i in range(1, n_sec - 1)])
    sent = pl.pallas_call(
        copies,
        out_shape=jax.ShapeDtypeStruct((n_sec // 2, M, M), BF16),
        in_specs=[VMEM],
        out_specs=VMEM,
        compiler_params=PARAMS,
        cost_estimate=pl.CostEstimate(flops=SPREAD_COST * M**3, bytes_accessed=1 << 20, transcendentals=0),
    )(right)
    sent, near = together(sent, near)
    inner = lax.ppermute(turned[H * M :], "sec", across)
    far = lax.ppermute(near[: H * M], "sec", across)
    right = lax.all_to_all(sent, "sec", 0, 0, axis_index_groups=by_core, tiled=True)
    payloads, inner, far = together(payloads, inner, far)
    other_payloads = lax.ppermute(payloads, "sec", across)

    own = pl.pallas_call(
        own_products,
        out_shape=jax.ShapeDtypeStruct((H, NW * M, M), BF16),
        in_specs=[VMEM] * 5,
        out_specs=VMEM,
        scratch_shapes=[pltpu.VMEM((4, H * M, M), BF16)],
        compiler_params=PARAMS,
        cost_estimate=pl.CostEstimate(flops=2 * 160 * M**3, bytes_accessed=3 << 20, transcendentals=0),
    )(payloads, near, turned, inner, far)
    results = pl.pallas_call(
        all_products,
        out_shape=jax.ShapeDtypeStruct((G, 2, M, M), BF16),
        in_specs=[SMEM] + [VMEM] * 7,
        out_specs=VMEM,
        scratch_shapes=[pltpu.VMEM((4, H * M, M), BF16), pltpu.VMEM((H, NW * M, M), BF16)],
        compiler_params=PARAMS,
        cost_estimate=pl.CostEstimate(flops=2 * 224 * M**3, bytes_accessed=6 << 20, transcendentals=0),
    )(allowed, other_payloads, near, turned, inner, far, right, own)

    received = lax.all_to_all(results, BOTH, 0, 0, axis_index_groups=exchange, tiled=True)
    A = s // G
    first = jnp.where(A < t, H, jnp.where(A > t, 0, lax.rem(A, 2) * H))
    return lax.dynamic_slice_in_dim(received, first, H, 0).reshape(G, 1, M, M)


def solution(mesh):
    in_specs = (
        P("sec", None, None, None),
        P("term", None, "sec", None, None),
        P("term", "sec", None, None),
        P("term", None, None, None),
        P("term", None),
        P(),
    )
    body = functools.partial(on_device, n_sec=mesh.shape["sec"], n_term=mesh.shape["term"])
    return jax.shard_map(
        body, mesh=mesh, in_specs=in_specs, out_specs=P("term", "sec", None, None), check_vma=False
    )
```

```python
import functools

import jax
import jax.numpy as jnp
from jax import lax
from jax.experimental import pallas as pl
from jax.experimental.pallas import tpu as pltpu
from jax.sharding import PartitionSpec as P

M = 128
LB = 5
NW = 8
G = 8
H = G // 2
BOTH = ("sec", "term")
ROWS = LB * M
F32 = jnp.float32
BF16 = jnp.bfloat16
VMEM = pl.BlockSpec(memory_space=pltpu.VMEM)
SMEM = pl.BlockSpec(memory_space=pltpu.SMEM)
PARAMS = pltpu.CompilerParams(vmem_limit_bytes=16 * 1024 * 1024)
FIRST = pltpu.CompilerParams(vmem_limit_bytes=56 * 1024 * 1024)
SPREAD_COST = 100


def together(*arrays):
    return lax.optimization_barrier(arrays)


def right_chip(t, w, i):
    ahead = (w - t) & 7
    far = ahead >> 2
    pair = far * (ahead - 4) + (1 - far) * (3 - ahead)
    x = ((t >> 1) + (pair ^ (pair >> 1))) & 3
    y = (4 * (t & 1) + far * (-1, 1, 2, 4)[i] + (1 - far) * (-2, 0, 3, 5)[i]) & 7
    return x * 8 + y


def pack(shift_ref, env_ref, coupling_ref, allowed_ref, payload_ref, table_ref):
    s = lax.axis_index("sec")
    n_sec = allowed_ref.shape[0]
    payload_ref[:ROWS, :] = env_ref[...]
    table_ref[...] = jnp.zeros_like(table_ref)
    lane = lax.broadcasted_iota(jnp.int32, (1, M), 1)
    shifts = jnp.zeros((1, M), F32)
    for c in range(LB):
        shift = shift_ref[0, c]
        source = s + shift
        inside = jnp.logical_and(source >= 0, source < n_sec).astype(F32)
        kept = allowed_ref[pl.ds(jnp.clip(source, 0, n_sec - 1), 1), :].astype(F32) * inside
        factor = coupling_ref[c, pl.ds(s, 1), :] * kept
        high = factor.astype(BF16).astype(F32)
        middle = (factor - high).astype(BF16).astype(F32)
        low = (factor - high - middle).astype(BF16).astype(F32)
        table_ref[c : c + 1, :] = jnp.concatenate([high, middle], axis=1)
        table_ref[8 + c : 9 + c, :n_sec] = low
        shifts = jnp.where(lane == c, shift.astype(F32), shifts)
    table_ref[15:16, :] = shifts
    payload_ref[ROWS:, :] = table_ref[...].astype(BF16)


def turn(psi_ref, turned_ref, block_ref, sem):
    copy = pltpu.make_async_copy(psi_ref.at[0, pl.ds(lax.axis_index("term") * G, G)], block_ref, sem)
    copy.start()
    copy.wait()
    for j in range(G):
        turned_ref[j * M : (j + 1) * M, :] = block_ref[j].T


def copies(block_ref, out_ref):
    for n in range(out_ref.shape[0]):
        out_ref[n] = block_ref[0]


def left_products(slots, below_ref, turned_ref, above_ref, out_ref, psi_ref):
    for row, ref in enumerate((below_ref, turned_ref, above_ref)):
        psi_ref[row] = ref[...]
    t = lax.axis_index("term")
    sector = lax.broadcasted_iota(jnp.int32, (M, G * M), 0)
    wanted = lax.broadcasted_iota(jnp.int32, (M, G * M), 1) // M + t * G
    pick = jnp.where((sector == wanted) | (sector == wanted + M // 2), 1.0, 0.0).astype(BF16)
    for w in range(H):
        table = slots[w, ROWS : ROWS + 16, :]
        spread = jnp.dot(table, pick, preferred_element_type=F32)
        factors = spread[:8] + spread[8:]
        shifts = table.astype(F32)[15:16, :]
        rows = [shifts[0, c].astype(jnp.int32) + 1 for c in range(LB)]
        for start in range(0, G * M, 2 * M):
            totals = [None, None]
            for c in range(LB):
                product = lax.dot_general(
                    psi_ref[rows[c], start : start + 2 * M, :],
                    slots[w, c * M : (c + 1) * M, :],
                    (((1,), (1,)), ((), ())),
                    preferred_element_type=F32,
                )
                for h in range(2):
                    at = start + h * M
                    term = product[h * M : (h + 1) * M] * factors[c : c + 1, at : at + M]
                    totals[h] = term if totals[h] is None else totals[h] + term
            for h in range(2):
                out_ref[start // M + h, w * M : (w + 1) * M, :] = totals[h].astype(BF16)


def right_sum(i, side, right_ref, same_ref, next_ref, allowed_ref):
    s, t = lax.axis_index("sec"), lax.axis_index("term")
    parity = lax.rem(t, 2)
    j = 2 * i + side
    same = jnp.concatenate([right_ref[right_chip(t, 2 * m + parity, i)] for m in range(H)], axis=1)
    following = jnp.concatenate([right_ref[right_chip(t, 2 * m + 1 - parity, i)] for m in range(H)], axis=1)
    total = jnp.dot(same, same_ref[j], preferred_element_type=F32)
    total += jnp.dot(following, next_ref[j], preferred_element_type=F32)
    return (total * allowed_ref[s, t * G + j].astype(F32)).T.astype(BF16)


def right_own(allowed_ref, right_ref, same_ref, next_ref, out_ref):
    core = lax.rem(lax.axis_index("sec"), 2)
    for i in range(H):
        out_ref[i] = right_sum(i, core, right_ref, same_ref, next_ref, allowed_ref)


def right_other(allowed_ref, right_ref, same_ref, next_ref, own_ref, out_ref):
    core = lax.rem(lax.axis_index("sec"), 2)
    for i in range(H):
        value = right_sum(i, 1 - core, right_ref, same_ref, next_ref, allowed_ref)
        out_ref[2 * i + 1 - core] = value
        out_ref[G + 2 * i + 1 - core] = value
        mine = own_ref[i]
        out_ref[2 * i + core] = mine
        out_ref[G + 2 * i + core] = mine


def on_device(wavefunction, left_env, right_env, coupling, left_shift, allowed, *, n_sec, n_term):
    s, t = lax.axis_index("sec"), lax.axis_index("term")
    groups = n_sec // G

    def device(sec, term):
        return sec * n_term + term

    spread = [
        (device(b, w), device(2 * right_chip(b // G, w, b % G // 2) + b % 2, b // G))
        for b in range(n_sec)
        for w in range(n_term)
    ]
    by_core = [[2 * chip + core for chip in range(n_sec // 2)] for core in range(2)]
    def members(A, B):
        return [device(A * G + i, B) for i in range(G)]

    exchange = [members(A, B) + members(B, A) for A in range(groups) for B in range(A + 1, groups)]
    exchange += [members(A, A) + members(A + 1, A + 1) for A in range(0, groups, 2)]

    right = lax.ppermute(right_env[0], BOTH, spread)
    payload = pl.pallas_call(
        pack,
        out_shape=jax.ShapeDtypeStruct((ROWS + 16, M), BF16),
        in_specs=[SMEM] + [VMEM] * 3,
        out_specs=VMEM,
        scratch_shapes=[pltpu.VMEM((16, M), F32)],
        compiler_params=FIRST,
    )(left_shift, left_env.reshape(ROWS, M), coupling[0], allowed)
    turned = pl.pallas_call(
        turn,
        out_shape=jax.ShapeDtypeStruct((G * M, M), BF16),
        in_specs=[pl.BlockSpec(memory_space=pl.ANY)],
        out_specs=VMEM,
        scratch_shapes=[pltpu.VMEM((G, M, M), BF16), pltpu.SemaphoreType.DMA],
        compiler_params=FIRST,
    )(wavefunction)

    below = lax.ppermute(turned, "sec", [(i, i + 1) for i in range(n_sec - 1)])
    above = lax.ppermute(turned, "sec", [(i + 1, i) for i in range(n_sec - 1)])
    sent = pl.pallas_call(
        copies,
        out_shape=jax.ShapeDtypeStruct((n_sec // 2, M, M), BF16),
        in_specs=[VMEM],
        out_specs=VMEM,
        compiler_params=PARAMS,
        cost_estimate=pl.CostEstimate(flops=SPREAD_COST * M**3, bytes_accessed=1 << 20, transcendentals=0),
    )(right)
    sent, below, above, payload = together(sent, below, above, payload)
    right = lax.all_to_all(sent, "sec", 0, 0, axis_index_groups=by_core, tiled=True)
    same = lax.all_gather(
        payload, "term", axis_index_groups=[list(range(parity, n_term, 2)) for parity in range(2)]
    )
    following = lax.ppermute(same, "term", [(i, i ^ 1) for i in range(n_term)])

    def left_call(slots):
        return pl.pallas_call(
            left_products,
            out_shape=jax.ShapeDtypeStruct((G, H * M, M), BF16),
            in_specs=[VMEM] * 4,
            out_specs=VMEM,
            scratch_shapes=[pltpu.VMEM((3, G * M, M), BF16)],
            compiler_params=PARAMS,
            cost_estimate=pl.CostEstimate(flops=2 * 160 * M**3, bytes_accessed=3 << 20, transcendentals=0),
        )(slots, below, turned, above)

    partial_same = left_call(same)
    following, partial_same, right = together(following, partial_same, right)
    partial_next = left_call(following)
    others = lax.ppermute(right, "sec", [(i, i ^ 1) for i in range(n_sec)])
    cost = pl.CostEstimate(flops=2 * 32 * M**3, bytes_accessed=2 << 20, transcendentals=0)
    own = pl.pallas_call(
        right_own,
        out_shape=jax.ShapeDtypeStruct((H, M, M), BF16),
        in_specs=[SMEM] + [VMEM] * 3,
        out_specs=VMEM,
        compiler_params=PARAMS,
        cost_estimate=cost,
    )(allowed, right, partial_same, partial_next)
    results = pl.pallas_call(
        right_other,
        out_shape=jax.ShapeDtypeStruct((2 * G, M, M), BF16),
        in_specs=[SMEM] + [VMEM] * 4,
        out_specs=VMEM,
        compiler_params=PARAMS,
        cost_estimate=cost,
    )(allowed, others, partial_same, partial_next, own)

    received = lax.all_to_all(results, BOTH, 0, 0, axis_index_groups=exchange, tiled=True)
    A = s // G
    first = jnp.where(A < t, G, jnp.where(A > t, 0, lax.rem(A, 2) * G))
    return lax.dynamic_slice_in_dim(received, first, G, 0)[:, None]


def solution(mesh):
    in_specs = (
        P("sec", None, None, None),
        P("term", None, "sec", None, None),
        P("term", "sec", None, None),
        P("term", None, None, None),
        P("term", None),
        P(),
    )
    body = functools.partial(on_device, n_sec=mesh.shape["sec"], n_term=mesh.shape["term"])
    return jax.shard_map(
        body, mesh=mesh, in_specs=in_specs, out_specs=P("term", "sec", None, None), check_vma=False
    )
```

```python
import functools

import jax
import jax.numpy as jnp
from jax import lax
from jax.experimental import pallas as pl
from jax.experimental.pallas import tpu as pltpu
from jax.sharding import PartitionSpec as P

M = 128
LB = 5
NW = 8
G = 8
H = G // 2
BOTH = ("sec", "term")
ROWS = LB * M
F32 = jnp.float32
BF16 = jnp.bfloat16
VMEM = pl.BlockSpec(memory_space=pltpu.VMEM)
SMEM = pl.BlockSpec(memory_space=pltpu.SMEM)
PARAMS = pltpu.CompilerParams(vmem_limit_bytes=16 * 1024 * 1024)
FIRST = pltpu.CompilerParams(vmem_limit_bytes=56 * 1024 * 1024)
SPREAD_COST = 100


def together(*arrays):
    return lax.optimization_barrier(arrays)


def right_chip(t, w, i):
    ahead = (w - t) & 7
    far = ahead >> 2
    pair = far * (ahead - 4) + (1 - far) * (3 - ahead)
    x = ((t >> 1) + (pair ^ (pair >> 1))) & 3
    y = (4 * (t & 1) + far * (-1, 1, 2, 4)[i] + (1 - far) * (-2, 0, 3, 5)[i]) & 7
    return x * 8 + y


def pack(shift_ref, env_ref, coupling_ref, allowed_ref, payload_ref, table_ref):
    s = lax.axis_index("sec")
    n_sec = allowed_ref.shape[0]
    payload_ref[:ROWS, :] = env_ref[...]
    table_ref[...] = jnp.zeros_like(table_ref)
    lane = lax.broadcasted_iota(jnp.int32, (1, M), 1)
    shifts = jnp.zeros((1, M), F32)
    for c in range(LB):
        shift = shift_ref[0, c]
        source = s + shift
        inside = jnp.logical_and(source >= 0, source < n_sec).astype(F32)
        kept = allowed_ref[pl.ds(jnp.clip(source, 0, n_sec - 1), 1), :].astype(F32) * inside
        factor = coupling_ref[c, pl.ds(s, 1), :] * kept
        high = factor.astype(BF16).astype(F32)
        middle = (factor - high).astype(BF16).astype(F32)
        low = (factor - high - middle).astype(BF16).astype(F32)
        table_ref[c : c + 1, :] = jnp.concatenate([high, middle], axis=1)
        table_ref[8 + c : 9 + c, :n_sec] = low
        shifts = jnp.where(lane == c, shift.astype(F32), shifts)
    table_ref[15:16, :] = shifts
    payload_ref[ROWS:, :] = table_ref[...].astype(BF16)


def turn(psi_ref, turned_ref, block_ref, sem):
    copy = pltpu.make_async_copy(psi_ref.at[0, pl.ds(lax.axis_index("term") * G, G)], block_ref, sem)
    copy.start()
    copy.wait()
    for j in range(G):
        turned_ref[j * M : (j + 1) * M, :] = block_ref[j].T


def copies(block_ref, out_ref):
    for n in range(out_ref.shape[0]):
        out_ref[n] = block_ref[0]


def left_products(count, *refs):
    below_ref, turned_ref, above_ref, out_ref, psi_ref = refs[count:]
    for row, ref in enumerate((below_ref, turned_ref, above_ref)):
        psi_ref[row] = ref[...]
    slots = [ref.at[w] for ref in refs[:count] for w in range(ref.shape[0])]
    t = lax.axis_index("term")
    sector = lax.broadcasted_iota(jnp.int32, (M, G * M), 0)
    wanted = lax.broadcasted_iota(jnp.int32, (M, G * M), 1) // M + t * G
    pick = jnp.where((sector == wanted) | (sector == wanted + M // 2), 1.0, 0.0).astype(BF16)
    for w, slot in enumerate(slots):
        table = slot[ROWS : ROWS + 16, :]
        spread = jnp.dot(table, pick, preferred_element_type=F32)
        factors = spread[:8] + spread[8:]
        shifts = table.astype(F32)[15:16, :]
        rows = [shifts[0, c].astype(jnp.int32) + 1 for c in range(LB)]
        for start in range(0, G * M, 2 * M):
            totals = [None, None]
            for c in range(LB):
                product = lax.dot_general(
                    psi_ref[rows[c], start : start + 2 * M, :],
                    slot[c * M : (c + 1) * M, :],
                    (((1,), (1,)), ((), ())),
                    preferred_element_type=F32,
                )
                for h in range(2):
                    at = start + h * M
                    term = product[h * M : (h + 1) * M] * factors[c : c + 1, at : at + M]
                    totals[h] = term if totals[h] is None else totals[h] + term
            for h in range(2):
                out_ref[start // M + h, w * M : (w + 1) * M, :] = totals[h].astype(BF16)


def right_sum(i, side, right_ref, same_ref, next_ref, allowed_ref):
    s, t = lax.axis_index("sec"), lax.axis_index("term")
    parity = lax.rem(t, 2)
    j = 2 * i + side
    same = jnp.concatenate([right_ref[right_chip(t, 2 * m + parity, i)] for m in range(H)], axis=1)
    following = jnp.concatenate([right_ref[right_chip(t, 2 * m + 1 - parity, i)] for m in range(H)], axis=1)
    total = jnp.dot(same, same_ref[j], preferred_element_type=F32)
    total += jnp.dot(following, next_ref[j], preferred_element_type=F32)
    return (total * allowed_ref[s, t * G + j].astype(F32)).T.astype(BF16)


def right_own(allowed_ref, right_ref, same_ref, next_ref, out_ref):
    core = lax.rem(lax.axis_index("sec"), 2)
    for i in range(H):
        out_ref[i] = right_sum(i, core, right_ref, same_ref, next_ref, allowed_ref)


def right_other(allowed_ref, right_ref, same_ref, next_ref, own_ref, out_ref):
    core = lax.rem(lax.axis_index("sec"), 2)
    for i in range(H):
        value = right_sum(i, 1 - core, right_ref, same_ref, next_ref, allowed_ref)
        out_ref[2 * i + 1 - core] = value
        out_ref[G + 2 * i + 1 - core] = value
        mine = own_ref[i]
        out_ref[2 * i + core] = mine
        out_ref[G + 2 * i + core] = mine


def on_device(wavefunction, left_env, right_env, coupling, left_shift, allowed, *, n_sec, n_term):
    s, t = lax.axis_index("sec"), lax.axis_index("term")
    groups = n_sec // G

    def device(sec, term):
        return sec * n_term + term

    spread = [
        (device(b, w), device(2 * right_chip(b // G, w, b % G // 2) + b % 2, b // G))
        for b in range(n_sec)
        for w in range(n_term)
    ]
    by_core = [[2 * chip + core for chip in range(n_sec // 2)] for core in range(2)]
    def members(A, B):
        return [device(A * G + i, B) for i in range(G)]

    exchange = [members(A, B) + members(B, A) for A in range(groups) for B in range(A + 1, groups)]
    exchange += [members(A, A) + members(A + 1, A + 1) for A in range(0, groups, 2)]

    right = lax.ppermute(right_env[0], BOTH, spread)
    payload = pl.pallas_call(
        pack,
        out_shape=jax.ShapeDtypeStruct((ROWS + 16, M), BF16),
        in_specs=[SMEM] + [VMEM] * 3,
        out_specs=VMEM,
        scratch_shapes=[pltpu.VMEM((16, M), F32)],
        compiler_params=FIRST,
    )(left_shift, left_env.reshape(ROWS, M), coupling[0], allowed)
    turned = pl.pallas_call(
        turn,
        out_shape=jax.ShapeDtypeStruct((G * M, M), BF16),
        in_specs=[pl.BlockSpec(memory_space=pl.ANY)],
        out_specs=VMEM,
        scratch_shapes=[pltpu.VMEM((G, M, M), BF16), pltpu.SemaphoreType.DMA],
        compiler_params=FIRST,
    )(wavefunction)

    below = lax.ppermute(turned, "sec", [(i, i + 1) for i in range(n_sec - 1)])
    above = lax.ppermute(turned, "sec", [(i + 1, i) for i in range(n_sec - 1)])
    sent = pl.pallas_call(
        copies,
        out_shape=jax.ShapeDtypeStruct((n_sec // 2, M, M), BF16),
        in_specs=[VMEM],
        out_specs=VMEM,
        compiler_params=PARAMS,
        cost_estimate=pl.CostEstimate(flops=SPREAD_COST * M**3, bytes_accessed=1 << 20, transcendentals=0),
    )(right)
    sent, below, above, payload = together(sent, below, above, payload)
    right = lax.all_to_all(sent, "sec", 0, 0, axis_index_groups=by_core, tiled=True)
    same = lax.all_gather(
        payload, "term", axis_index_groups=[list(range(parity, n_term, 2)) for parity in range(2)]
    )
    from_below = lax.ppermute(same[: H // 2], "term", [(i, (i + 1) % n_term) for i in range(n_term)])
    from_above = lax.ppermute(same[H // 2 :], "term", [(i, (i - 1) % n_term) for i in range(n_term)])

    def left_call(*slots):
        return pl.pallas_call(
            functools.partial(left_products, len(slots)),
            out_shape=jax.ShapeDtypeStruct((G, H * M, M), BF16),
            in_specs=[VMEM] * (len(slots) + 3),
            out_specs=VMEM,
            scratch_shapes=[pltpu.VMEM((3, G * M, M), BF16)],
            compiler_params=PARAMS,
            cost_estimate=pl.CostEstimate(flops=2 * 160 * M**3, bytes_accessed=3 << 20, transcendentals=0),
        )(*slots, below, turned, above)

    partial_same = left_call(same)
    from_below, from_above, partial_same, right = together(from_below, from_above, partial_same, right)
    partial_next = left_call(from_below, from_above)
    others = lax.ppermute(right, "sec", [(i, i ^ 1) for i in range(n_sec)])
    cost = pl.CostEstimate(flops=2 * 32 * M**3, bytes_accessed=2 << 20, transcendentals=0)
    own = pl.pallas_call(
        right_own,
        out_shape=jax.ShapeDtypeStruct((H, M, M), BF16),
        in_specs=[SMEM] + [VMEM] * 3,
        out_specs=VMEM,
        compiler_params=PARAMS,
        cost_estimate=cost,
    )(allowed, right, partial_same, partial_next)
    results = pl.pallas_call(
        right_other,
        out_shape=jax.ShapeDtypeStruct((2 * G, M, M), BF16),
        in_specs=[SMEM] + [VMEM] * 4,
        out_specs=VMEM,
        compiler_params=PARAMS,
        cost_estimate=cost,
    )(allowed, others, partial_same, partial_next, own)

    received = lax.all_to_all(results, BOTH, 0, 0, axis_index_groups=exchange, tiled=True)
    A = s // G
    first = jnp.where(A < t, G, jnp.where(A > t, 0, lax.rem(A, 2) * G))
    return lax.dynamic_slice_in_dim(received, first, G, 0)[:, None]


def solution(mesh):
    in_specs = (
        P("sec", None, None, None),
        P("term", None, "sec", None, None),
        P("term", "sec", None, None),
        P("term", None, None, None),
        P("term", None),
        P(),
    )
    body = functools.partial(on_device, n_sec=mesh.shape["sec"], n_term=mesh.shape["term"])
    return jax.shard_map(
        body, mesh=mesh, in_specs=in_specs, out_specs=P("term", "sec", None, None), check_vma=False
    )
```

```python
import functools

import jax
import jax.numpy as jnp
from jax import lax
from jax.experimental import pallas as pl
from jax.experimental.pallas import tpu as pltpu
from jax.sharding import PartitionSpec as P

M = 128
LB = 5
NW = 8
G = 8
H = G // 2
BOTH = ("sec", "term")
ROWS = LB * M
F32 = jnp.float32
BF16 = jnp.bfloat16
VMEM = pl.BlockSpec(memory_space=pltpu.VMEM)
SMEM = pl.BlockSpec(memory_space=pltpu.SMEM)
PARAMS = pltpu.CompilerParams(vmem_limit_bytes=16 * 1024 * 1024)
FIRST = pltpu.CompilerParams(vmem_limit_bytes=56 * 1024 * 1024)
SPREAD_COST = 100


def together(*arrays):
    return lax.optimization_barrier(arrays)


def right_chip(t, w, i):
    ahead = (w - t) & 7
    far = ahead >> 2
    pair = far * (ahead - 4) + (1 - far) * (3 - ahead)
    x = ((t >> 1) + (pair ^ (pair >> 1))) & 3
    y = (4 * (t & 1) + far * (-1, 1, 2, 4)[i] + (1 - far) * (-2, 0, 3, 5)[i]) & 7
    return x * 8 + y


def pack(shift_ref, env_ref, coupling_ref, allowed_ref, payload_ref, table_ref):
    s = lax.axis_index("sec")
    n_sec = allowed_ref.shape[0]
    payload_ref[:ROWS, :] = env_ref[...]
    table_ref[...] = jnp.zeros_like(table_ref)
    lane = lax.broadcasted_iota(jnp.int32, (1, M), 1)
    shifts = jnp.zeros((1, M), F32)
    for c in range(LB):
        shift = shift_ref[0, c]
        source = s + shift
        inside = jnp.logical_and(source >= 0, source < n_sec).astype(F32)
        kept = allowed_ref[pl.ds(jnp.clip(source, 0, n_sec - 1), 1), :].astype(F32) * inside
        factor = coupling_ref[c, pl.ds(s, 1), :] * kept
        high = factor.astype(BF16).astype(F32)
        middle = (factor - high).astype(BF16).astype(F32)
        low = (factor - high - middle).astype(BF16).astype(F32)
        table_ref[c : c + 1, :] = jnp.concatenate([high, middle], axis=1)
        table_ref[8 + c : 9 + c, :n_sec] = low
        shifts = jnp.where(lane == c, shift.astype(F32), shifts)
    table_ref[15:16, :] = shifts
    payload_ref[ROWS:, :] = table_ref[...].astype(BF16)


def turn(psi_ref, turned_ref, block_ref, sem):
    copy = pltpu.make_async_copy(psi_ref.at[0, pl.ds(lax.axis_index("term") * G, G)], block_ref, sem)
    copy.start()
    copy.wait()
    for j in range(G):
        turned_ref[j * M : (j + 1) * M, :] = block_ref[j].T


def copies(block_ref, out_ref):
    for n in range(out_ref.shape[0]):
        out_ref[n] = block_ref[0]


def left_products(count, *refs):
    near_ref, turned_ref, inner_ref, out_ref, psi_ref = refs[count:]
    for row, ref in enumerate((near_ref, turned_ref, inner_ref)):
        psi_ref[row] = ref[...]
    slots = [ref.at[w] for ref in refs[:count] for w in range(ref.shape[0])]
    t = lax.axis_index("term")
    step = 1 - 2 * lax.rem(lax.axis_index("sec"), 2)
    sector = lax.broadcasted_iota(jnp.int32, (M, G * M), 0)
    wanted = lax.broadcasted_iota(jnp.int32, (M, G * M), 1) // M + t * G
    pick = jnp.where((sector == wanted) | (sector == wanted + M // 2), 1.0, 0.0).astype(BF16)
    for w, slot in enumerate(slots):
        table = slot[ROWS : ROWS + 16, :]
        spread = jnp.dot(table, pick, preferred_element_type=F32)
        factors = spread[:8] + spread[8:]
        shifts = table.astype(F32)[15:16, :]
        rows = [shifts[0, c].astype(jnp.int32) * step + 1 for c in range(LB)]
        for start in range(0, G * M, 2 * M):
            totals = [None, None]
            for c in range(LB):
                product = lax.dot_general(
                    psi_ref[rows[c], start : start + 2 * M, :],
                    slot[c * M : (c + 1) * M, :],
                    (((1,), (1,)), ((), ())),
                    preferred_element_type=F32,
                )
                for h in range(2):
                    at = start + h * M
                    term = product[h * M : (h + 1) * M] * factors[c : c + 1, at : at + M]
                    totals[h] = term if totals[h] is None else totals[h] + term
            for h in range(2):
                out_ref[start // M + h, w * M : (w + 1) * M, :] = totals[h].astype(BF16)


def right_sum(i, side, right_ref, same_ref, next_ref, allowed_ref):
    s, t = lax.axis_index("sec"), lax.axis_index("term")
    parity = lax.rem(t, 2)
    j = 2 * i + side
    same = jnp.concatenate([right_ref[right_chip(t, 2 * m + parity, i)] for m in range(H)], axis=1)
    following = jnp.concatenate([right_ref[right_chip(t, 2 * m + 1 - parity, i)] for m in range(H)], axis=1)
    total = jnp.dot(same, same_ref[j], preferred_element_type=F32)
    total += jnp.dot(following, next_ref[j], preferred_element_type=F32)
    return (total * allowed_ref[s, t * G + j].astype(F32)).T.astype(BF16)


def next_products(allowed_ref, *refs):
    left_refs, (right_ref, same_ref, next_ref, out_ref, psi_ref) = refs[:5], refs[5:]
    left_products(2, *left_refs, next_ref, psi_ref)
    core = lax.rem(lax.axis_index("sec"), 2)
    for i in range(H):
        out_ref[i] = right_sum(i, core, right_ref, same_ref, next_ref, allowed_ref)


def other_products(allowed_ref, right_ref, same_ref, next_ref, own_ref, out_ref):
    core = lax.rem(lax.axis_index("sec"), 2)
    for i in range(H):
        value = right_sum(i, 1 - core, right_ref, same_ref, next_ref, allowed_ref)
        out_ref[2 * i + 1 - core] = value
        out_ref[G + 2 * i + 1 - core] = value
        mine = own_ref[i]
        out_ref[2 * i + core] = mine
        out_ref[G + 2 * i + core] = mine


def on_device(wavefunction, left_env, right_env, coupling, left_shift, allowed, *, n_sec, n_term):
    s, t = lax.axis_index("sec"), lax.axis_index("term")
    groups = n_sec // G

    def device(sec, term):
        return sec * n_term + term

    spread = [
        (device(b, w), device(2 * right_chip(b // G, w, b % G // 2) + b % 2, b // G))
        for b in range(n_sec)
        for w in range(n_term)
    ]
    by_core = [[2 * chip + core for chip in range(n_sec // 2)] for core in range(2)]
    def members(A, B):
        return [device(A * G + i, B) for i in range(G)]

    exchange = [members(A, B) + members(B, A) for A in range(groups) for B in range(A + 1, groups)]
    exchange += [members(A, A) + members(A + 1, A + 1) for A in range(0, groups, 2)]

    right = lax.ppermute(right_env[0], BOTH, spread)
    payload = pl.pallas_call(
        pack,
        out_shape=jax.ShapeDtypeStruct((ROWS + 16, M), BF16),
        in_specs=[SMEM] + [VMEM] * 3,
        out_specs=VMEM,
        scratch_shapes=[pltpu.VMEM((16, M), F32)],
        compiler_params=FIRST,
    )(left_shift, left_env.reshape(ROWS, M), coupling[0], allowed)
    turned = pl.pallas_call(
        turn,
        out_shape=jax.ShapeDtypeStruct((G * M, M), BF16),
        in_specs=[pl.BlockSpec(memory_space=pl.ANY)],
        out_specs=VMEM,
        scratch_shapes=[pltpu.VMEM((G, M, M), BF16), pltpu.SemaphoreType.DMA],
        compiler_params=FIRST,
    )(wavefunction)

    near = lax.ppermute(turned, "sec", [(i, i + 1) if i % 2 else (i, i - 1) for i in range(1, n_sec - 1)])
    sent = pl.pallas_call(
        copies,
        out_shape=jax.ShapeDtypeStruct((n_sec // 2, M, M), BF16),
        in_specs=[VMEM],
        out_specs=VMEM,
        compiler_params=PARAMS,
        cost_estimate=pl.CostEstimate(flops=SPREAD_COST * M**3, bytes_accessed=1 << 20, transcendentals=0),
    )(right)
    sent, near, payload = together(sent, near, payload)
    right = lax.all_to_all(sent, "sec", 0, 0, axis_index_groups=by_core, tiled=True)
    same = lax.all_gather(
        payload, "term", axis_index_groups=[list(range(parity, n_term, 2)) for parity in range(2)]
    )
    across = [(i, i ^ 1) for i in range(n_sec)]
    inner = lax.ppermute(turned, "sec", across)
    from_below = lax.ppermute(same[: H // 2], "term", [(i, (i + 1) % n_term) for i in range(n_term)])
    from_above = lax.ppermute(same[H // 2 :], "term", [(i, (i - 1) % n_term) for i in range(n_term)])

    partial_same = pl.pallas_call(
        functools.partial(left_products, 1),
        out_shape=jax.ShapeDtypeStruct((G, H * M, M), BF16),
        in_specs=[VMEM] * 4,
        out_specs=VMEM,
        scratch_shapes=[pltpu.VMEM((3, G * M, M), BF16)],
        compiler_params=PARAMS,
        cost_estimate=pl.CostEstimate(flops=2 * 160 * M**3, bytes_accessed=3 << 20, transcendentals=0),
    )(same, near, turned, inner)
    from_below, from_above, partial_same, right = together(from_below, from_above, partial_same, right)
    others = lax.ppermute(right, "sec", across)
    cost = pl.CostEstimate(flops=2 * 112 * M**3, bytes_accessed=3 << 20, transcendentals=0)
    partial_next, own = pl.pallas_call(
        next_products,
        out_shape=[jax.ShapeDtypeStruct((G, H * M, M), BF16), jax.ShapeDtypeStruct((H, M, M), BF16)],
        in_specs=[SMEM] + [VMEM] * 7,
        out_specs=[VMEM] * 2,
        scratch_shapes=[pltpu.VMEM((3, G * M, M), BF16)],
        compiler_params=PARAMS,
        cost_estimate=cost,
    )(allowed, from_below, from_above, near, turned, inner, right, partial_same)
    results = pl.pallas_call(
        other_products,
        out_shape=jax.ShapeDtypeStruct((2 * G, M, M), BF16),
        in_specs=[SMEM] + [VMEM] * 4,
        out_specs=VMEM,
        compiler_params=PARAMS,
        cost_estimate=cost,
    )(allowed, others, partial_same, partial_next, own)

    received = lax.all_to_all(results, BOTH, 0, 0, axis_index_groups=exchange, tiled=True)
    A = s // G
    first = jnp.where(A < t, G, jnp.where(A > t, 0, lax.rem(A, 2) * G))
    return lax.dynamic_slice_in_dim(received, first, G, 0)[:, None]


def solution(mesh):
    in_specs = (
        P("sec", None, None, None),
        P("term", None, "sec", None, None),
        P("term", "sec", None, None),
        P("term", None, None, None),
        P("term", None),
        P(),
    )
    body = functools.partial(on_device, n_sec=mesh.shape["sec"], n_term=mesh.shape["term"])
    return jax.shard_map(
        body, mesh=mesh, in_specs=in_specs, out_specs=P("term", "sec", None, None), check_vma=False
    )
```

```python
import functools

import jax
import jax.numpy as jnp
from jax import lax
from jax.experimental import pallas as pl
from jax.experimental.pallas import tpu as pltpu
from jax.sharding import PartitionSpec as P

M = 128
LB = 5
NW = 8
G = 8
H = G // 2
BOTH = ("sec", "term")
ROWS = LB * M
F32 = jnp.float32
BF16 = jnp.bfloat16
VMEM = pl.BlockSpec(memory_space=pltpu.VMEM)
SMEM = pl.BlockSpec(memory_space=pltpu.SMEM)
PARAMS = pltpu.CompilerParams(vmem_limit_bytes=16 * 1024 * 1024)
FIRST = pltpu.CompilerParams(vmem_limit_bytes=56 * 1024 * 1024)
WEIGHTS = (4000, 8000)
SPREAD_COST = 100


def together(*arrays):
    return lax.optimization_barrier(arrays)


def right_chip(t, w, i):
    ahead = (w - t) & 7
    far = ahead >> 2
    pair = far * (ahead - 4) + (1 - far) * (3 - ahead)
    x = ((t >> 1) + (pair ^ (pair >> 1))) & 3
    y = (4 * (t & 1) + far * (-1, 1, 2, 4)[i] + (1 - far) * (-2, 0, 3, 5)[i]) & 7
    return x * 8 + y


def pack(shift_ref, env_ref, coupling_ref, allowed_ref, payload_ref, table_ref):
    s = lax.axis_index("sec")
    n_sec = allowed_ref.shape[0]
    payload_ref[:ROWS, :] = env_ref[...]
    table_ref[...] = jnp.zeros_like(table_ref)
    lane = lax.broadcasted_iota(jnp.int32, (1, M), 1)
    shifts = jnp.zeros((1, M), F32)
    result = allowed_ref[pl.ds(s, 1), :].astype(F32)
    for c in range(LB):
        shift = shift_ref[0, c]
        source = s + shift
        inside = jnp.logical_and(source >= 0, source < n_sec).astype(F32)
        kept = allowed_ref[pl.ds(jnp.clip(source, 0, n_sec - 1), 1), :].astype(F32) * inside * result
        factor = coupling_ref[c, pl.ds(s, 1), :] * kept
        high = factor.astype(BF16).astype(F32)
        middle = (factor - high).astype(BF16).astype(F32)
        low = (factor - high - middle).astype(BF16).astype(F32)
        table_ref[c : c + 1, :] = jnp.concatenate([high, middle], axis=1)
        table_ref[8 + c : 9 + c, :n_sec] = low
        shifts = jnp.where(lane == c, shift.astype(F32), shifts)
    table_ref[15:16, :] = shifts
    payload_ref[ROWS:, :] = table_ref[...].astype(BF16)


def turn(psi_ref, turned_ref, block_ref, sem):
    copy = pltpu.make_async_copy(psi_ref.at[0, pl.ds(lax.axis_index("term") * G, G)], block_ref, sem)
    copy.start()
    copy.wait()
    for j in range(G):
        turned_ref[j * M : (j + 1) * M, :] = block_ref[j].T


def copies(block_ref, out_ref):
    for n in range(out_ref.shape[0]):
        out_ref[n] = block_ref[0]


def left_products(count, *refs):
    near_ref, turned_ref, inner_ref, out_ref, psi_ref = refs[count:]
    for row, ref in enumerate((near_ref, turned_ref, inner_ref)):
        psi_ref[row] = ref[...]
    slots = [ref.at[w] for ref in refs[:count] for w in range(ref.shape[0])]
    t = lax.axis_index("term")
    step = 1 - 2 * lax.rem(lax.axis_index("sec"), 2)
    sector = lax.broadcasted_iota(jnp.int32, (M, G * M), 0)
    wanted = lax.broadcasted_iota(jnp.int32, (M, G * M), 1) // M + t * G
    pick = jnp.where((sector == wanted) | (sector == wanted + M // 2), 1.0, 0.0).astype(BF16)
    for w, slot in enumerate(slots):
        table = slot[ROWS : ROWS + 16, :]
        spread = jnp.dot(table, pick, preferred_element_type=F32)
        factors = spread[:8] + spread[8:]
        shifts = table.astype(F32)[15:16, :]
        rows = [shifts[0, c].astype(jnp.int32) * step + 1 for c in range(LB)]
        for start in range(0, G * M, 2 * M):
            totals = [None, None]
            for c in range(LB):
                product = lax.dot_general(
                    psi_ref[rows[c], start : start + 2 * M, :],
                    slot[c * M : (c + 1) * M, :],
                    (((1,), (1,)), ((), ())),
                    preferred_element_type=F32,
                )
                for h in range(2):
                    at = start + h * M
                    term = product[h * M : (h + 1) * M] * factors[c : c + 1, at : at + M]
                    totals[h] = term if totals[h] is None else totals[h] + term
            for h in range(2):
                out_ref[start // M + h, w * M : (w + 1) * M, :] = totals[h].astype(BF16)


def right_products(right_ref, others_ref, same_ref, next_ref, out_ref):
    t = lax.axis_index("term")
    core = lax.rem(lax.axis_index("sec"), 2)
    parity = lax.rem(t, 2)
    for ref, side in ((right_ref, core), (others_ref, 1 - core)):
        for i in range(H):
            j = 2 * i + side
            same = jnp.concatenate([ref[right_chip(t, 2 * m + parity, i)] for m in range(H)], axis=1)
            following = jnp.concatenate([ref[right_chip(t, 2 * m + 1 - parity, i)] for m in range(H)], axis=1)
            total = jnp.dot(same, same_ref[j], preferred_element_type=F32)
            total += jnp.dot(following, next_ref[j], preferred_element_type=F32)
            value = total.T.astype(BF16)
            out_ref[j] = value
            out_ref[G + j] = value


def on_device(wavefunction, left_env, right_env, coupling, left_shift, allowed, *, n_sec, n_term):
    s, t = lax.axis_index("sec"), lax.axis_index("term")
    groups = n_sec // G

    def device(sec, term):
        return sec * n_term + term

    spread = [
        (device(b, w), device(2 * right_chip(b // G, w, b % G // 2) + b % 2, b // G))
        for b in range(n_sec)
        for w in range(n_term)
    ]
    by_core = [[2 * chip + core for chip in range(n_sec // 2)] for core in range(2)]
    def members(A, B):
        return [device(A * G + i, B) for i in range(G)]

    exchange = [members(A, B) + members(B, A) for A in range(groups) for B in range(A + 1, groups)]
    exchange += [members(A, A) + members(A + 1, A + 1) for A in range(0, groups, 2)]

    right = lax.ppermute(right_env[0], BOTH, spread)
    payload = pl.pallas_call(
        pack,
        out_shape=jax.ShapeDtypeStruct((ROWS + 16, M), BF16),
        in_specs=[SMEM] + [VMEM] * 3,
        out_specs=VMEM,
        scratch_shapes=[pltpu.VMEM((16, M), F32)],
        compiler_params=FIRST,
    )(left_shift, left_env.reshape(ROWS, M), coupling[0], allowed)
    turned = pl.pallas_call(
        turn,
        out_shape=jax.ShapeDtypeStruct((G * M, M), BF16),
        in_specs=[pl.BlockSpec(memory_space=pl.ANY)],
        out_specs=VMEM,
        scratch_shapes=[pltpu.VMEM((G, M, M), BF16), pltpu.SemaphoreType.DMA],
        compiler_params=FIRST,
    )(wavefunction)

    near = lax.ppermute(turned, "sec", [(i, i + 1) if i % 2 else (i, i - 1) for i in range(1, n_sec - 1)])
    sent = pl.pallas_call(
        copies,
        out_shape=jax.ShapeDtypeStruct((n_sec // 2, M, M), BF16),
        in_specs=[VMEM],
        out_specs=VMEM,
        compiler_params=PARAMS,
        cost_estimate=pl.CostEstimate(flops=SPREAD_COST * M**3, bytes_accessed=1 << 20, transcendentals=0),
    )(right)
    sent, near, payload = together(sent, near, payload)
    right = lax.all_to_all(sent, "sec", 0, 0, axis_index_groups=by_core, tiled=True)
    same = lax.all_gather(
        payload, "term", axis_index_groups=[list(range(parity, n_term, 2)) for parity in range(2)]
    )
    across = [(i, i ^ 1) for i in range(n_sec)]
    inner = lax.ppermute(turned, "sec", across)
    from_below = lax.ppermute(same[: H // 2], "term", [(i, (i + 1) % n_term) for i in range(n_term)])
    from_above = lax.ppermute(same[H // 2 :], "term", [(i, (i - 1) % n_term) for i in range(n_term)])

    def left_call(weight, *slots):
        return pl.pallas_call(
            functools.partial(left_products, len(slots)),
            out_shape=jax.ShapeDtypeStruct((G, H * M, M), BF16),
            in_specs=[VMEM] * (len(slots) + 3),
            out_specs=VMEM,
            scratch_shapes=[pltpu.VMEM((3, G * M, M), BF16)],
            compiler_params=PARAMS,
            cost_estimate=pl.CostEstimate(flops=weight * M**3, bytes_accessed=3 << 20, transcendentals=0),
        )(*slots, near, turned, inner)

    partial_same = left_call(WEIGHTS[0], same)
    right, partial_same = together(right, partial_same)
    others = lax.ppermute(right, "sec", across)
    partial_next = left_call(WEIGHTS[1], from_below, from_above)
    results = pl.pallas_call(
        right_products,
        out_shape=jax.ShapeDtypeStruct((2 * G, M, M), BF16),
        in_specs=[VMEM] * 4,
        out_specs=VMEM,
        compiler_params=PARAMS,
        cost_estimate=pl.CostEstimate(flops=2 * 64 * M**3, bytes_accessed=3 << 20, transcendentals=0),
    )(right, others, partial_same, partial_next)

    received = lax.all_to_all(results, BOTH, 0, 0, axis_index_groups=exchange, tiled=True)
    A = s // G
    first = jnp.where(A < t, G, jnp.where(A > t, 0, lax.rem(A, 2) * G))
    return lax.dynamic_slice_in_dim(received, first, G, 0)[:, None]


def solution(mesh):
    in_specs = (
        P("sec", None, None, None),
        P("term", None, "sec", None, None),
        P("term", "sec", None, None),
        P("term", None, None, None),
        P("term", None),
        P(),
    )
    body = functools.partial(on_device, n_sec=mesh.shape["sec"], n_term=mesh.shape["term"])
    return jax.shard_map(
        body, mesh=mesh, in_specs=in_specs, out_specs=P("term", "sec", None, None), check_vma=False
    )
```

```python
import functools

import jax
import jax.numpy as jnp
from jax import lax
from jax.experimental import pallas as pl
from jax.experimental.pallas import tpu as pltpu
from jax.sharding import PartitionSpec as P

M = 128
LB = 5
NW = 8
G = 8
H = G // 2
BOTH = ("sec", "term")
ROWS = LB * M
F32 = jnp.float32
BF16 = jnp.bfloat16
VMEM = pl.BlockSpec(memory_space=pltpu.VMEM)
SMEM = pl.BlockSpec(memory_space=pltpu.SMEM)
PARAMS = pltpu.CompilerParams(vmem_limit_bytes=16 * 1024 * 1024)
FIRST = pltpu.CompilerParams(vmem_limit_bytes=56 * 1024 * 1024)
WEIGHTS = (4000, 8000)
SPREAD_COST = 100


def together(*arrays):
    return lax.optimization_barrier(arrays)


def right_chip(t, w, i):
    ahead = (w - t) & 7
    far = ahead >> 2
    pair = far * (ahead - 4) + (1 - far) * (3 - ahead)
    x = ((t >> 1) + (pair ^ (pair >> 1))) & 3
    y = (4 * (t & 1) + far * (-1, 1, 2, 4)[i] + (1 - far) * (-2, 0, 3, 5)[i]) & 7
    return x * 8 + y


def pack(shift_ref, env_ref, coupling_ref, allowed_ref, payload_ref, table_ref):
    s = lax.axis_index("sec")
    n_sec = allowed_ref.shape[0]
    payload_ref[:ROWS, :] = env_ref[...]
    table_ref[...] = jnp.zeros_like(table_ref)
    lane = lax.broadcasted_iota(jnp.int32, (1, M), 1)
    shifts = jnp.zeros((1, M), F32)
    result = allowed_ref[pl.ds(s, 1), :].astype(F32)
    for c in range(LB):
        shift = shift_ref[0, c]
        source = s + shift
        inside = jnp.logical_and(source >= 0, source < n_sec).astype(F32)
        kept = allowed_ref[pl.ds(jnp.clip(source, 0, n_sec - 1), 1), :].astype(F32) * inside * result
        factor = coupling_ref[c, pl.ds(s, 1), :] * kept
        high = factor.astype(BF16).astype(F32)
        middle = (factor - high).astype(BF16).astype(F32)
        low = (factor - high - middle).astype(BF16).astype(F32)
        table_ref[c : c + 1, :] = jnp.concatenate([high, middle], axis=1)
        table_ref[8 + c : 9 + c, :n_sec] = low
        shifts = jnp.where(lane == c, shift.astype(F32), shifts)
    table_ref[15:16, :] = shifts
    payload_ref[ROWS:, :] = table_ref[...].astype(BF16)


def turn(psi_ref, turned_ref, block_ref, sem):
    copy = pltpu.make_async_copy(psi_ref.at[0, pl.ds(lax.axis_index("term") * G, G)], block_ref, sem)
    copy.start()
    copy.wait()
    for j in range(G):
        turned_ref[j * M : (j + 1) * M, :] = block_ref[j].T


def copies(block_ref, out_ref):
    for n in range(out_ref.shape[0]):
        out_ref[n] = block_ref[0]


def left_products(count, *refs):
    near_ref, turned_ref, inner_ref, out_ref, psi_ref = refs[count:]
    for row, ref in enumerate((near_ref, turned_ref, inner_ref)):
        psi_ref[row] = ref[...]
    slots = [ref.at[w] for ref in refs[:count] for w in range(ref.shape[0])]
    t = lax.axis_index("term")
    step = 1 - 2 * lax.rem(lax.axis_index("sec"), 2)
    sector = lax.broadcasted_iota(jnp.int32, (M, G * M), 0)
    wanted = lax.broadcasted_iota(jnp.int32, (M, G * M), 1) // M + t * G
    pick = jnp.where((sector == wanted) | (sector == wanted + M // 2), 1.0, 0.0).astype(BF16)
    for w, slot in enumerate(slots):
        table = slot[ROWS : ROWS + 16, :]
        spread = jnp.dot(table, pick, preferred_element_type=F32)
        factors = spread[:8] + spread[8:]
        shifts = table.astype(F32)[15:16, :]
        rows = [shifts[0, c].astype(jnp.int32) * step + 1 for c in range(LB)]
        for start in range(0, G * M, 2 * M):
            totals = [None, None]
            for c in range(LB):
                product = lax.dot_general(
                    psi_ref[rows[c], start : start + 2 * M, :],
                    slot[c * M : (c + 1) * M, :],
                    (((1,), (1,)), ((), ())),
                    preferred_element_type=F32,
                )
                for h in range(2):
                    at = start + h * M
                    term = product[h * M : (h + 1) * M] * factors[c : c + 1, at : at + M]
                    totals[h] = term if totals[h] is None else totals[h] + term
            for h in range(2):
                out_ref[start // M + h, w * M : (w + 1) * M, :] = totals[h].astype(BF16)


def right_products(right_ref, others_ref, same_ref, next_ref, out_ref):
    t = lax.axis_index("term")
    core = lax.rem(lax.axis_index("sec"), 2)
    parity = lax.rem(t, 2)
    for ref, side in ((right_ref, core), (others_ref, 1 - core)):
        for i in range(H):
            j = 2 * i + side
            same = jnp.concatenate([ref[right_chip(t, 2 * m + parity, i)] for m in range(H)], axis=1)
            following = jnp.concatenate([ref[right_chip(t, 2 * m + 1 - parity, i)] for m in range(H)], axis=1)
            total = jnp.dot(same, same_ref[j], preferred_element_type=F32)
            total += jnp.dot(following, next_ref[j], preferred_element_type=F32)
            value = total.T.astype(BF16)
            out_ref[j] = value
            out_ref[G + j] = value


def on_device(wavefunction, left_env, right_env, coupling, left_shift, allowed, *, n_sec, n_term):
    s, t = lax.axis_index("sec"), lax.axis_index("term")
    groups = n_sec // G

    def device(sec, term):
        return sec * n_term + term

    spread = [
        (device(b, w), device(2 * right_chip(b // G, w, b % G // 2) + b % 2, b // G))
        for b in range(n_sec)
        for w in range(n_term)
    ]
    by_core = [[2 * chip + core for chip in range(n_sec // 2)] for core in range(2)]
    def members(A, B):
        return [device(A * G + i, B) for i in range(G)]

    exchange = [members(A, B) + members(B, A) for A in range(groups) for B in range(A + 1, groups)]
    exchange += [members(A, A) + members(A + 1, A + 1) for A in range(0, groups, 2)]

    right = lax.ppermute(right_env[0], BOTH, spread)
    payload = pl.pallas_call(
        pack,
        out_shape=jax.ShapeDtypeStruct((ROWS + 16, M), BF16),
        in_specs=[SMEM] + [VMEM] * 3,
        out_specs=VMEM,
        scratch_shapes=[pltpu.VMEM((16, M), F32)],
        compiler_params=FIRST,
    )(left_shift, left_env.reshape(ROWS, M), coupling[0], allowed)
    turned = pl.pallas_call(
        turn,
        out_shape=jax.ShapeDtypeStruct((G * M, M), BF16),
        in_specs=[pl.BlockSpec(memory_space=pl.ANY)],
        out_specs=VMEM,
        scratch_shapes=[pltpu.VMEM((G, M, M), BF16), pltpu.SemaphoreType.DMA],
        compiler_params=FIRST,
    )(wavefunction)

    near = lax.ppermute(turned, "sec", [(i, i + 1) if i % 2 else (i, i - 1) for i in range(1, n_sec - 1)])
    sent = pl.pallas_call(
        copies,
        out_shape=jax.ShapeDtypeStruct((n_sec // 2, M, M), BF16),
        in_specs=[VMEM],
        out_specs=VMEM,
        compiler_params=PARAMS,
        cost_estimate=pl.CostEstimate(flops=SPREAD_COST * M**3, bytes_accessed=1 << 20, transcendentals=0),
    )(right)
    sent, near, payload = together(sent, near, payload)
    right = lax.all_to_all(sent, "sec", 0, 0, axis_index_groups=by_core, tiled=True)
    same = lax.all_gather(
        payload, "term", axis_index_groups=[list(range(parity, n_term, 2)) for parity in range(2)]
    )
    across = [(i, i ^ 1) for i in range(n_sec)]
    same, late = together(same, turned)
    inner = lax.ppermute(late, "sec", across)
    from_below = lax.ppermute(same[: H // 2], "term", [(i, (i + 1) % n_term) for i in range(n_term)])
    from_above = lax.ppermute(same[H // 2 :], "term", [(i, (i - 1) % n_term) for i in range(n_term)])

    def left_call(weight, *slots):
        return pl.pallas_call(
            functools.partial(left_products, len(slots)),
            out_shape=jax.ShapeDtypeStruct((G, H * M, M), BF16),
            in_specs=[VMEM] * (len(slots) + 3),
            out_specs=VMEM,
            scratch_shapes=[pltpu.VMEM((3, G * M, M), BF16)],
            compiler_params=PARAMS,
            cost_estimate=pl.CostEstimate(flops=weight * M**3, bytes_accessed=3 << 20, transcendentals=0),
        )(*slots, near, turned, inner)

    partial_same = left_call(WEIGHTS[0], same)
    right, partial_same = together(right, partial_same)
    others = lax.ppermute(right, "sec", across)
    partial_next = left_call(WEIGHTS[1], from_below, from_above)
    results = pl.pallas_call(
        right_products,
        out_shape=jax.ShapeDtypeStruct((2 * G, M, M), BF16),
        in_specs=[VMEM] * 4,
        out_specs=VMEM,
        compiler_params=PARAMS,
        cost_estimate=pl.CostEstimate(flops=2 * 64 * M**3, bytes_accessed=3 << 20, transcendentals=0),
    )(right, others, partial_same, partial_next)

    received = lax.all_to_all(results, BOTH, 0, 0, axis_index_groups=exchange, tiled=True)
    A = s // G
    first = jnp.where(A < t, G, jnp.where(A > t, 0, lax.rem(A, 2) * G))
    return lax.dynamic_slice_in_dim(received, first, G, 0)[:, None]


def solution(mesh):
    in_specs = (
        P("sec", None, None, None),
        P("term", None, "sec", None, None),
        P("term", "sec", None, None),
        P("term", None, None, None),
        P("term", None),
        P(),
    )
    body = functools.partial(on_device, n_sec=mesh.shape["sec"], n_term=mesh.shape["term"])
    return jax.shard_map(
        body, mesh=mesh, in_specs=in_specs, out_specs=P("term", "sec", None, None), check_vma=False
    )
```
